256 devices in a mesh: ctx: 32 (over x, z), head: 2 (over core), dp: 4 (over y).
Axes of the slice: x: 4, y: 4, z: 8, core: 2. Of those that a mesh axis runs over, the one named last changes fastest.
Arguments:
- enc_query: bfloat16 [32768, 2048], P(('dp', 'ctx'), 'head'), parts along dimension 0, may hold values from -24 to 24
- enc_key: bfloat16 [32768, 2048], P(('dp', 'ctx'), 'head'), parts along dimension 0, may hold values from -24 to 24
- enc_value: bfloat16 [32768, 2048], P(('dp', 'ctx'), 'head'), parts along dimension 0, may hold values from -6 to 6
- input_segments: int32 [32768], P(('dp', 'ctx')), parts along dimension 0, may hold values from 0 to 7, as said below
- doc_bounds: int32 [128, 2], P(('dp', 'ctx')), parts along dimension 0, may hold values from 0 to 8192, as said below
- target_query: bfloat16 [4096, 2048], P(('dp', 'ctx'), 'head'), parts along dimension 0, may hold values from -24 to 24
- cross_key: bfloat16 [32768, 2048], P(('dp', 'ctx'), 'head'), parts along dimension 0, may hold values from -24 to 24
- cross_value: bfloat16 [32768, 2048], P(('dp', 'ctx'), 'head'), parts along dimension 0, may hold values from -6 to 6
- target_segments: int32 [4096], P('dp'), parts along dimension 0, may hold values from 0 to 7, as said below
Outputs:
- enc_out: bfloat16 [32768, 2048], P(('dp', 'ctx'), 'head'), parts along dimension 0
- cross_out: bfloat16 [4096, 2048], P(('dp', 'ctx'), 'head'), parts along dimension 0
The draws below stay inside these ranges and needn't reach their ends.
There are 4 independent parts, one for each index of `dp`. The reference program is written for one: setup_inputs(seed, part) draws one part's arguments, and reference() takes and returns one part's arrays. A program takes and returns all parts, laid end to end along the dimension named above; each array names one. Nothing has to cross between parts.
Inputs may be any that keep to these rules, and one draw needn't show every extreme that they name: `input_segments`: ids never fall along the slots; each of the 8 documents holds at least one slot, and one holds exactly 6144 slots. `target_segments`: ids never fall along the slots; each of the 8 documents has at least one target slot. `doc_bounds`: row b holds the first slot of the document of input slot b * 256 and one past the last slot of the document of input slot (b + 1) * 256 - 1, as input_segments gives them.
All inputs are finite; a program needn't handle non-finite values.
Results may differ from the reference program's by a relative error of at most 0.005.
Values may be sent and summed in bfloat16 or wider, within the bound.
No kernel may reach another device: no remote copies, remote signals or barrier semaphores. Data moves between devices by JAX's collectives and lax.ppermute only.
A program may use at most 192 MiB of HBM per device.

```python
import jax
import jax.numpy as jnp
from jax import lax

HEADS = 8
HEAD_DIM = 256
TOK_DEV = 256
NDOCS = 8
TOKENS = 8192
TARGETS = 1024


def noise(key, rows, scale):
    return scale * jnp.clip(jax.random.normal(key, (rows, HEADS, HEAD_DIM), jnp.float32), -6.0, 6.0)


def flatten(base):
    return base.reshape(base.shape[0], HEADS * HEAD_DIM).astype(jnp.bfloat16)


def draw_enc_query(key, part):
    key = jax.random.fold_in(key, 3)
    base = noise(key, TOKENS, 2.5)
    return flatten(base)


def draw_enc_key(key, part):
    key = jax.random.fold_in(key, 4)
    base = noise(key, TOKENS, 1.0)
    return flatten(base)


def draw_target_query(key, part):
    key = jax.random.fold_in(key, 6)
    base = noise(key, TARGETS, 2.5)
    return flatten(base)


def draw_cross_key(key, part):
    key = jax.random.fold_in(key, 7)
    base = noise(key, TOKENS, 1.0)
    return flatten(base)


def documents(key):
    rest = TOKENS - 3 * TOKENS // 4
    cuts = jnp.sort(jax.random.permutation(jax.random.fold_in(key, 11), rest - 1)[:NDOCS - 2] + 1)
    edges = jnp.concatenate([jnp.zeros((1,), jnp.int32), cuts.astype(jnp.int32), jnp.full((1,), rest, jnp.int32)])
    small = edges[1:] - edges[:-1]
    big_at = jax.random.randint(jax.random.fold_in(key, 12), (), 0, NDOCS)
    order = jnp.arange(NDOCS)
    source = jnp.clip(jnp.where(order < big_at, order, order - 1), 0, NDOCS - 2)
    lengths = jnp.where(order == big_at, 3 * TOKENS // 4, small[source]).astype(jnp.int32)
    ends = jnp.cumsum(lengths).astype(jnp.int32)
    starts = ends - lengths
    positions = jnp.arange(TOKENS)
    segments = jnp.sum((positions[:, None] >= ends[None, :]).astype(jnp.int32), axis=1).astype(jnp.int32)
    return (segments, starts, ends)


def draw_input_segments(key, part):
    segments, starts, ends = documents(key)
    return segments


def draw_doc_bounds(key, part):
    segments, starts, ends = documents(key)
    first_ids = segments[::TOK_DEV]
    last_ids = segments[TOK_DEV - 1::TOK_DEV]
    order = jnp.arange(NDOCS)
    begin = jnp.sum(jnp.where(first_ids[:, None] == order[None, :], starts[None, :], 0), axis=1)
    finish = jnp.sum(jnp.where(last_ids[:, None] == order[None, :], ends[None, :], 0), axis=1)
    return jnp.stack([begin, finish], axis=1).astype(jnp.int32)


def draw_target_segments(key, part):
    key = jax.random.fold_in(key, 5)
    cuts = jax.random.permutation(key, TARGETS - 1)[:NDOCS - 1] + 1
    positions = jnp.arange(TARGETS)
    return jnp.sum((positions[:, None] >= cuts[None, :]).astype(jnp.int32), axis=1).astype(jnp.int32)


def level_of(own_key, extent, shards, low, high):
    factor_of = 1.0
    for dim, shards_of in shards:
        steps = jax.random.uniform(jax.random.fold_in(jax.random.fold_in(own_key, 6), dim), (shards_of,), jnp.float32, low / len(shards), high / len(shards))
        factor_of = factor_of * jnp.repeat(jnp.exp(steps), extent[dim] // shards_of).reshape((-1,) + (1,) * (len(extent) - 1 - dim))
    return factor_of


def bell_draw(key, shape, scale, reach, shards=(), kind=jnp.bfloat16):
    values = scale * jax.random.normal(key, shape, jnp.float32)
    if shards:
        values = values * level_of(key, shape, shards, -0.22, 0.18)
    return jnp.clip(values, -reach, reach).astype(kind)


def setup_inputs(seed: int = 0, part: int = 0) -> dict:
    splits = jax.random.split(jax.random.key(seed), 10)
    part_splits = jax.random.split(jax.random.fold_in(splits[9], part), 10)
    enc_query = draw_enc_query(jax.random.fold_in(jax.random.fold_in(splits[9], part), 71), part)
    enc_key = draw_enc_key(jax.random.fold_in(jax.random.fold_in(splits[9], part), 71), part)
    enc_value = bell_draw(part_splits[2], (TOKENS, HEADS * HEAD_DIM), 1.0, 6.0, ((0, 32), (1, 2)))
    input_segments = draw_input_segments(jax.random.fold_in(jax.random.fold_in(splits[9], part), 71), part)
    doc_bounds = draw_doc_bounds(jax.random.fold_in(jax.random.fold_in(splits[9], part), 71), part)
    target_query = draw_target_query(jax.random.fold_in(jax.random.fold_in(splits[9], part), 71), part)
    cross_key = draw_cross_key(jax.random.fold_in(jax.random.fold_in(splits[9], part), 71), part)
    cross_value = bell_draw(part_splits[7], (TOKENS, HEADS * HEAD_DIM), 1.0, 6.0, ((0, 32), (1, 2)))
    target_segments = draw_target_segments(jax.random.fold_in(jax.random.fold_in(splits[9], part), 71), part)
    return dict(enc_query=enc_query, enc_key=enc_key, enc_value=enc_value, input_segments=input_segments, doc_bounds=doc_bounds, target_query=target_query, cross_key=cross_key, cross_value=cross_value, target_segments=target_segments)


def attend_heads(query, keys, values, allowed):
    rows = query.shape[0]
    heads = query.shape[1] // HEAD_DIM
    query3 = query.reshape(rows, heads, HEAD_DIM).transpose(1, 0, 2)
    keys3 = keys.reshape(keys.shape[0], heads, HEAD_DIM).transpose(1, 0, 2)
    values3 = values.reshape(values.shape[0], heads, HEAD_DIM).transpose(1, 0, 2)

    def one_head(triple):
        head_query, head_keys, head_values = triple
        scores = jnp.dot(head_query, head_keys.T, preferred_element_type=jnp.float32) * (HEAD_DIM ** -0.5)
        scores = jnp.where(allowed, scores, -1.0e30)
        top = jnp.max(scores, axis=1, keepdims=True)
        weights = jnp.where(allowed, jnp.exp(scores - top), 0.0)
        summed = jnp.dot(weights.astype(jnp.bfloat16), head_values, preferred_element_type=jnp.float32)
        return summed / jnp.sum(weights, axis=1, keepdims=True)

    result = lax.map(one_head, (query3, keys3, values3))
    return result.transpose(1, 0, 2).reshape(rows, heads * HEAD_DIM).astype(jnp.bfloat16)


def reference(enc_query, enc_key, enc_value, input_segments, doc_bounds, target_query, cross_key, cross_value, target_segments):
    positions = jnp.arange(TOKENS, dtype=jnp.int32)
    lower = jnp.repeat(doc_bounds[:, 0], TOK_DEV)
    upper = jnp.repeat(doc_bounds[:, 1], TOK_DEV)
    self_allowed = (input_segments[:, None] == input_segments[None, :])
    self_allowed = self_allowed & (positions[None, :] >= lower[:, None]) & (positions[None, :] < upper[:, None])
    enc_out = attend_heads(enc_query, enc_key, enc_value, self_allowed)
    cross_allowed = target_segments[:, None] == input_segments[None, :]
    cross_out = attend_heads(target_query, cross_key, cross_value, cross_allowed)
    return (enc_out, cross_out)
```

```python
import functools

import jax
import jax.numpy as jnp
from jax import lax
from jax.experimental import pallas as pl
from jax.experimental.pallas import tpu as pltpu
from jax.sharding import Mesh
from jax.sharding import PartitionSpec as P

HEAD_DIM = 256
HALF = 128
TGT = 32
NEG = -1.0e30
LOW = -1.0e29

ROW_V = HALF
ROW_ID = 2 * HALF
ROW_Q = ROW_ID + 16
ROW_T = ROW_Q + HALF
ROW_XK = ROW_T + TGT
ROW_XV = ROW_XK + HALF
ROWS = ROW_XV + HALF
STEPS = 8
WIDE = HEAD_DIM + 128
LIMIT = 40 * 1024 * 1024


def z_pairs(k):
    d, t = k % 4, k // 4
    return [
        (z * 2 + c, (4 * c + (z + d) % 4) * 2 + (t ^ (z // 4))) for z in range(8) for c in range(2)
    ]


def z_send(array, k):
    return lax.ppermute(array, ("z", "core"), z_pairs(k))


def z_return(array, k):
    return lax.ppermute(array, ("z", "core"), [(b, a) for a, b in z_pairs(k)])


def x_send(array, shift):
    return lax.ppermute(array, "x", [(i, (i + shift) % 4) for i in range(4)])


def xc_send(array, shift, swap):
    pairs = [
        (x * 2 + c, ((x + shift) % 4) * 2 + (c ^ swap)) for x in range(4) for c in range(2)
    ]
    return lax.ppermute(array, ("x", "core"), pairs)


def core_swap(array):
    return lax.ppermute(array, "core", [(0, 1), (1, 0)])


def params(flops, moved):
    return dict(
        compiler_params=pltpu.CompilerParams(vmem_limit_bytes=LIMIT),
        cost_estimate=pl.CostEstimate(flops=flops, bytes_accessed=moved, transcendentals=0),
    )


def pack_kernel(z_ref, k_ref, v_ref, id_ref, q_ref, t_ref, xk_ref, xv_ref, *outs):
    z = z_ref[0]
    for k in range(STEPS):
        d, t = k % 4, k // 4
        col = pl.ds(pl.multiple_of(lax.rem(z + d, 4) * HEAD_DIM, HEAD_DIM), HEAD_DIM)
        half = lax.rem(t + z // 4, 2)
        row = pl.ds(pl.multiple_of(half * HALF, HALF), HALF)
        out = outs[k]
        out[0:ROW_V, :] = k_ref[row, col]
        out[ROW_V:ROW_ID, :] = v_ref[row, col]
        out[ROW_ID:ROW_Q, :] = id_ref[half]
        out[ROW_Q:ROW_T, :] = q_ref[row, col] * jnp.bfloat16(HEAD_DIM**-0.5)
        out[ROW_T:ROW_XK, :] = t_ref[:, col] * jnp.bfloat16(HEAD_DIM**-0.5)
        out[ROW_XK:ROW_XV, :] = xk_ref[row, col]
        out[ROW_XV:ROWS, :] = xv_ref[row, col]


def pack(z, keys, values, ids, query, target, cross_keys, cross_values):
    whole = pl.BlockSpec(memory_space=pltpu.VMEM)
    return pl.pallas_call(
        pack_kernel,
        out_shape=[jax.ShapeDtypeStruct((ROWS, HEAD_DIM), jnp.bfloat16)] * STEPS,
        in_specs=[pl.BlockSpec(memory_space=pltpu.SMEM)] + [whole] * 7,
        out_specs=[whole] * STEPS,
        **params(0, 6 * 1024 * 1024),
    )(z, keys, values, ids, query, target, cross_keys, cross_values)


def unpack_kernel(z_ref, *refs):
    z = z_ref[0]
    outs = refs[STEPS + 4 :]
    for k in range(STEPS):
        d, t = k % 4, k // 4
        col = pl.ds(pl.multiple_of(lax.rem(z + d, 4) * HEAD_DIM, HEAD_DIM), HEAD_DIM)
        half = lax.rem(t + z // 4, 2)
        row = pl.ds(pl.multiple_of(half * HALF, HALF), HALF)
        outs[0][row, col] = refs[k][...]
        if t == 0:
            outs[1][:, col] = refs[STEPS + d][...]


def unpack(z, pieces, cross_pieces):
    whole = pl.BlockSpec(memory_space=pltpu.VMEM)
    return pl.pallas_call(
        unpack_kernel,
        out_shape=[
            jax.ShapeDtypeStruct((2 * HALF, 4 * HEAD_DIM), jnp.bfloat16),
            jax.ShapeDtypeStruct((TGT, 4 * HEAD_DIM), jnp.bfloat16),
        ],
        in_specs=[pl.BlockSpec(memory_space=pltpu.SMEM)] + [whole] * (STEPS + 4),
        out_specs=[whole] * 2,
        **params(0, 1024 * 1024),
    )(z, *pieces, *cross_pieces)


def attend_kernel(layout, key_rows, q_row, has_ids, has_carry, final, partner, *refs):
    refs = list(refs)
    q_ref = refs.pop(0)
    id_ref = refs.pop(0) if has_ids else None
    key_refs = [refs.pop(0) for _ in layout]
    carry_ref = refs.pop(0) if has_carry else None
    other_ref = refs.pop(0) if partner else None
    out_ref = refs.pop(0)
    k_row, v_row = key_rows
    pieces = []
    for ref, count in zip(key_refs, layout, strict=True):
        pieces += [ref] if count is None else [ref.at[i] for i in range(count)]
    keys = jnp.concatenate([p[k_row : k_row + HALF, :] for p in pieces], axis=0)
    values = jnp.concatenate([p[v_row : v_row + HALF, :] for p in pieces], axis=0)
    key_ids = [p[ROW_ID : ROW_ID + 16, 0:128].astype(jnp.float32)[0:1, :] for p in pieces]
    for sub in range(2):
        rows = slice(sub * 256, sub * 256 + 256)
        query = q_ref[2 * sub : 2 * sub + 2, q_row : q_row + HALF, :].reshape(256, HEAD_DIM)
        columns = []
        for chunk in (2 * sub, 2 * sub + 1):
            if has_ids:
                row = id_ref[chunk, 0:1, :]
            else:
                row = q_ref[chunk, 0:16, 0:128].astype(jnp.float32)[0:1, :]
            columns.append(jnp.transpose(jnp.broadcast_to(row, (128, 128))))
        query_ids = jnp.concatenate(columns, axis=0)
        match = jnp.concatenate([query_ids == ids for ids in key_ids], axis=1)
        scores = lax.dot_general(
            query, keys, (((1,), (1,)), ((), ())), preferred_element_type=jnp.float32
        )
        scores = jnp.where(match, scores, NEG)
        top = jnp.max(scores, axis=1, keepdims=True)
        if has_carry:
            old = carry_ref[rows, HEAD_DIM : HEAD_DIM + 1]
            top = jnp.maximum(top, old)
        else:
            top = jnp.maximum(top, LOW)
        weights = jnp.exp(scores - top)
        total = jnp.sum(weights, axis=1, keepdims=True)
        summed = jnp.dot(
            weights.astype(jnp.bfloat16), values, preferred_element_type=jnp.float32
        )
        if has_carry:
            scale = jnp.exp(old - top)
            total = total + scale * carry_ref[rows, HEAD_DIM + 64 : HEAD_DIM + 65]
            summed = summed + scale * carry_ref[rows, 0:HEAD_DIM]
        if final:
            some = total > 0.0
            safe = jnp.where(some, total, 1.0)
            summed = summed / safe
            level = jnp.where(some, top + jnp.log(safe), NEG)
            if partner:
                other = other_ref[rows, HEAD_DIM : HEAD_DIM + 1]
                both = jnp.maximum(level, other)
                mine, theirs = jnp.exp(level - both), jnp.exp(other - both)
                summed = (mine * summed + theirs * other_ref[rows, 0:HEAD_DIM]) / (mine + theirs)
                out_ref[rows, :] = summed.astype(jnp.bfloat16)
            else:
                out_ref[rows, 0:HEAD_DIM] = summed
                out_ref[rows, HEAD_DIM:WIDE] = jnp.broadcast_to(level, (256, 128))
        else:
            lane = lax.broadcasted_iota(jnp.int32, (256, 128), 1)
            out_ref[rows, 0:HEAD_DIM] = summed
            out_ref[rows, HEAD_DIM:WIDE] = jnp.where(lane < 64, top, total)


def attend(query, q_row, ids, keys, key_rows, carry=None, final=False, other=None):
    def fixed(array):
        return pl.BlockSpec(array.shape, lambda i, n=array.ndim: (0,) * n)

    operands = [query]
    specs = [pl.BlockSpec((4,) + query.shape[1:], lambda i: (i, 0, 0))]
    if ids is not None:
        operands.append(ids)
        specs.append(pl.BlockSpec((4,) + ids.shape[1:], lambda i: (i, 0, 0)))
    for array in keys:
        operands.append(array)
        specs.append(fixed(array))
    for array in (carry, other):
        if array is not None:
            operands.append(array)
            specs.append(pl.BlockSpec((512, WIDE), lambda i: (i, 0)))
    if other is None:
        out, out_spec = jax.ShapeDtypeStruct((1024, WIDE), jnp.float32), (512, WIDE)
    else:
        out, out_spec = jax.ShapeDtypeStruct((1024, HEAD_DIM), jnp.bfloat16), (512, HEAD_DIM)
    layout = tuple(None if a.ndim == 2 else a.shape[0] for a in keys)
    return pl.pallas_call(
        functools.partial(
            attend_kernel, layout, key_rows, q_row, ids is not None, carry is not None, final, other is not None
        ),
        out_shape=out,
        grid=(2,),
        in_specs=specs,
        out_specs=pl.BlockSpec(out_spec, lambda i: (i, 0)),
        **params(4 * 1024 * 1024 * HEAD_DIM, 8 * 1024 * 1024),
    )(*operands)


def merge_kernel(*refs):
    out_ref = refs[-1]
    levels = [ref[:, HEAD_DIM : HEAD_DIM + 1] for ref in refs[:-1]]
    top = functools.reduce(jnp.maximum, levels)
    shares = [jnp.exp(level - top) for level in levels]
    summed = sum(share * ref[:, 0:HEAD_DIM] for share, ref in zip(shares, refs[:-1], strict=True))
    out_ref[...] = (summed / sum(shares)).astype(jnp.bfloat16)


def merge(parts):
    whole = pl.BlockSpec(memory_space=pltpu.VMEM)
    return pl.pallas_call(
        merge_kernel,
        out_shape=jax.ShapeDtypeStruct((HALF, HEAD_DIM), jnp.bfloat16),
        in_specs=[whole] * len(parts),
        out_specs=whole,
        **params(0, 2 * 1024 * 1024),
    )(*parts)


def per_device(
    enc_query,
    enc_key,
    enc_value,
    input_segments,
    doc_bounds,
    target_query,
    cross_key,
    cross_value,
    target_segments,
):
    del doc_bounds
    ix, iz, ic = lax.axis_index("x"), lax.axis_index("z"), lax.axis_index("core")
    place = iz.astype(jnp.int32).reshape(1)
    ids = jnp.tile(
        jnp.broadcast_to(input_segments.reshape(2, 1, HALF).astype(jnp.bfloat16), (2, 16, HALF)), (1, 1, 2)
    )
    steps = jnp.arange(STEPS)
    from_z = (iz - steps % 4) % 4 + 4 * ((steps // 4) ^ ic)
    from_x = (ix + jnp.array([0, 3, 1, 2])) % 4
    order = (from_x[:, None] * 8 + from_z[None, :]).reshape(32)
    pick = (order[:, None] == jnp.arange(32)[None, :]).astype(jnp.float32)
    target_ids = jnp.dot(pick, target_segments.reshape(32, TGT).astype(jnp.float32))
    target_ids = jnp.broadcast_to(target_ids.reshape(8, 1, 128), (8, 8, 128))

    sent = pack(place, enc_key, enc_value, ids, enc_query, target_query, cross_key, cross_value)
    got = [z_send(sent[k], k) for k in range(STEPS)]

    mine = jnp.stack([g[ROW_ID:ROW_T] for g in got])
    theirs = core_swap(mine)

    groups = [jnp.stack([g[:ROW_Q] for g in got[i : i + 4]]) for i in (0, 4)]
    left = [x_send(g, 1) for g in groups]
    right = [x_send(g, 3) for g in groups]
    far = [x_send(g[:2], 1) for g in left] + [x_send(g[2:], 3) for g in right]

    row_queries = jnp.concatenate([g[ROW_T:ROW_XK] for g in got], axis=0)
    queries = jnp.concatenate([row_queries] + [x_send(row_queries, s) for s in (1, 3, 2)], axis=0)
    part = attend(
        queries.reshape(8, HALF, HEAD_DIM), 0, target_ids, got, (ROW_XK, ROW_XV), final=True
    )
    parts = [part[0:HALF]]
    for shift, block in ((0, 0), (3, 1), (1, 2), (2, 3)):
        rows = part[block * 256 : block * 256 + 256]
        if shift:
            parts.append(xc_send(rows[:HALF], shift, 0))
        parts.append(xc_send(rows[HALF:], shift, 1))
    merged = merge(parts)
    cross_pieces = [z_return(merged[d * TGT : (d + 1) * TGT], d) for d in range(4)]

    enc = (0, ROW_V)
    carry = [None, None]
    for keys in (got, [left[0], right[0]], [left[1], right[1]]):
        carry = [attend(q, 16, None, keys, enc, carry=c) for q, c in zip((theirs, mine), carry)]
    partial = core_swap(attend(theirs, 16, None, far, enc, carry=carry[0], final=True))
    done = attend(mine, 16, None, far, enc, carry=carry[1], final=True, other=partial)
    pieces = [z_return(done[k * HALF : (k + 1) * HALF], k) for k in range(STEPS)]
    return tuple(unpack(place, pieces, cross_pieces))


def solution(mesh):
    shape = mesh.shape
    split = Mesh(
        mesh.devices.reshape(4, shape["ctx"] // 4, shape["head"], shape["dp"]), ("x", "z", "core", "dp")
    )
    tokens = P(("dp", "x", "z"), "core")
    placed = (
        tokens,
        tokens,
        tokens,
        P(("dp", "x", "z")),
        P(("dp", "x", "z"), None),
        tokens,
        tokens,
        tokens,
        P("dp"),
    )
    return jax.shard_map(
        per_device, mesh=split, in_specs=placed, out_specs=(tokens, tokens), check_vma=False
    )
```

```python
import functools

import jax
import jax.numpy as jnp
from jax import lax
from jax.experimental import pallas as pl
from jax.experimental.pallas import tpu as pltpu
from jax.sharding import Mesh
from jax.sharding import PartitionSpec as P

HEAD_DIM = 256
HALF = 128
TGT = 32
NEG = -1.0e30
LOW = -1.0e29

ROW_V = HALF
ROW_ID = 2 * HALF
ROW_Q = ROW_ID + 16
ROWS = ROW_Q + HALF
KEYS = ROW_Q
ASK = ROWS - ROW_ID
X_V = 2 * HALF
X_ID = 4 * HALF
X_T = X_ID + 16
X_ROWS = X_T + TGT
ORDER = (0, 3, 5, 1, 7, 2, 6, 4)
X_ORDER = (0, 1, 3, 2)
WIDE = HEAD_DIM + 128
MIB = 1024 * 1024
HALF_TYPE = jnp.bfloat16


def z_send(array, shift):
    return lax.ppermute(array, "z", [(i, (i + shift) % 8) for i in range(8)])


def x_send(array, shift):
    return lax.ppermute(array, "x", [(i, (i + shift) % 4) for i in range(4)])


def core_swap(array):
    return lax.ppermute(array, "core", [(0, 1), (1, 0)])


def params(flops, moved, limit=8):
    return dict(
        compiler_params=pltpu.CompilerParams(vmem_limit_bytes=limit * MIB),
        cost_estimate=pl.CostEstimate(flops=flops, bytes_accessed=moved, transcendentals=0),
    )


def rows_at(start, size, unit):
    return pl.ds(pl.multiple_of(start * unit, unit), size)


def half_rows(c):
    return rows_at(c, HALF, HALF)


def columns(j):
    return pl.ds(j * HEAD_DIM, HEAD_DIM)


def whole():
    return pl.BlockSpec(memory_space=pltpu.VMEM)


def scalars():
    return pl.BlockSpec(memory_space=pltpu.SMEM)


def shaped(*shape):
    return jax.ShapeDtypeStruct(shape, HALF_TYPE)


def copy(a, b):
    b[...] = a[...]


def copies(place, plan, ins, outs, after=()):
    def kernel(place_ref, *refs):
        at = (place_ref[0], place_ref[1], place_ref[2])
        for a, b, *when in plan(at, refs[: len(ins)], refs[len(ins) + len(after) :]):
            if when:
                pl.when(when[0])(functools.partial(copy, a, b))
            else:
                copy(a, b)

    return pl.pallas_call(
        kernel,
        out_shape=[shaped(*shape) for shape in outs],
        in_specs=[scalars()] + [whole()] * len(ins) + [pl.BlockSpec(memory_space=pl.ANY)] * len(after),
        out_specs=[whole()] * len(outs),
        **params(0, 2 * MIB),
    )(place, *ins, *after)


def named(number_ref, half):
    row = number_ref[pl.ds(half, 1), :].astype(jnp.float32)
    return jnp.broadcast_to(row, (16, HALF)).astype(HALF_TYPE)


def load(place, keys, values, query, target, cross_keys, cross_values, numbers):
    def kernel(place_ref, k_ref, v_ref, q_ref, t_ref, xk_ref, xv_ref, id_ref, near, away, heads, sems):
        c = place_ref[1]
        made = []
        for side, out in ((1 - c, away), (c, near)):
            for i, ref in enumerate((k_ref, v_ref, q_ref)):
                made.append((ref.at[half_rows(side)], out.at[pl.ds(i * HALF, HALF)]))
        for j in range(4):
            for ref, row, size in ((xk_ref, 0, 2 * HALF), (xv_ref, X_V, 2 * HALF), (t_ref, X_T, TGT)):
                made.append((ref.at[:, columns(j)], heads.at[j, pl.ds(row, size)]))
        made = [pltpu.make_async_copy(a, b, sems.at[i]) for i, (a, b) in enumerate(made)]
        for one in made:
            one.start()
        for j in range(4):
            for half in (0, 1):
                heads[j, X_ID:X_T, half * HALF : half * HALF + HALF] = named(id_ref, half)
        for one in made:
            one.wait()

    return pl.pallas_call(
        kernel,
        out_shape=[shaped(3 * HALF, 4 * HEAD_DIM)] * 2 + [shaped(4, X_ROWS, HEAD_DIM)],
        in_specs=[scalars()] + [pl.BlockSpec(memory_space=pl.ANY)] * 6 + [whole()],
        out_specs=[whole()] * 3,
        scratch_shapes=[pltpu.SemaphoreType.DMA((18,))],
        **params(0, 6 * MIB, 56),
    )(place, keys, values, query, target, cross_keys, cross_values, numbers)


class Either:
    def __init__(self, first, a, b):
        self.first, self.a, self.b = first, a, b

    def __getitem__(self, key):
        return jnp.where(self.first, self.a[key], self.b[key])


class Row:
    def __init__(self, ref, half):
        self.ref, self.half = ref, half

    def __getitem__(self, key):
        row = named(self.ref, self.half)
        return jnp.concatenate([row, row], axis=1)


def plan_pack(shifts, at, ins, outs):
    z, c, _ = at
    near, swapped, ids = ins
    pairs = []
    for k, d in enumerate(shifts):
        head = lax.rem(z + d, 8)
        column = rows_at(lax.rem(head, 4), HEAD_DIM, HEAD_DIM)
        first = (head // 4) == c
        for i, row in enumerate((0, ROW_V, ROW_Q)):
            part = (pl.ds(i * HALF, HALF), column)
            pairs.append((Either(first, near.at[part], swapped.at[part]), outs[k].at[pl.ds(row, HALF)]))
        pairs.append((Row(ids, c), outs[k].at[pl.ds(ROW_ID, 16)]))
    return pairs


def plan_first(at, ins, outs):
    group, ask = outs
    pairs = []
    for i, ref in enumerate(ins):
        pairs.append((ref.at[pl.ds(0, KEYS)], group.at[i]))
        pairs.append((ref.at[pl.ds(ROW_ID, ASK)], ask.at[i]))
    return pairs


def plan_second(at, ins, outs):
    chunks, (left, right, ask_first) = ins[:3], ins[3:]
    to_right, to_left, ask = outs
    pairs = [
        (left.at[pl.ds(0, 3)], to_right.at[pl.ds(0, 3)]),
        (right.at[pl.ds(3, 2)], to_left.at[pl.ds(0, 2)]),
        (ask_first, ask.at[pl.ds(0, 5)]),
    ]
    for i, ref in enumerate(chunks):
        pairs.append((ref.at[pl.ds(0, KEYS)], to_right.at[3 + i]))
        pairs.append((ref.at[pl.ds(0, KEYS)], to_left.at[2 + i]))
        pairs.append((ref.at[pl.ds(ROW_ID, ASK)], ask.at[5 + i]))
    return pairs


def plan_third(at, ins, outs):
    return [(ins[0].at[pl.ds(3, 1)], outs[0]), (ins[1].at[pl.ds(3, 2)], outs[1])]


def plan_targets(at, ins, outs):
    return [
        (ins[0].at[x, pl.ds(X_T, TGT)], outs[0].at[z, pl.ds(x * TGT, TGT)]) for x in range(4) for z in range(8)
    ]


def plan_back(at, ins, outs):
    z = at[0]
    return [
        (ins[0].at[pl.ds(k * HALF, HALF)], outs[0].at[lax.rem(z + 8 - d, 8)]) for k, d in enumerate(ORDER)
    ]


def plan_cross_back(at, ins, outs):
    x = at[2]
    return [
        (ins[0].at[rows_at(lax.rem(x + 4 - d, 4), TGT, TGT)], out) for d, out in zip(X_ORDER, outs, strict=True)
    ]


def plan_back_swap(at, ins, outs):
    return [(ins[0].at[pl.ds(4 * (1 - at[1]), 4)], outs[0])]


def plan_unpack(at, ins, outs):
    c = at[1]
    pairs = []
    back, swapped = ins[:2]
    for j in range(4):
        pairs.append((back.at[4 * c + j], outs[0].at[half_rows(c), columns(j)]))
        pairs.append((swapped.at[j], outs[0].at[half_rows(1 - c), columns(j)]))
    return pairs


def plan_cross_unpack(at, ins, outs):
    pairs = []
    for piece, shift in zip(ins, X_ORDER, strict=True):
        column = rows_at(lax.rem(at[2] + shift, 4), HEAD_DIM, HEAD_DIM)
        pairs.append((piece, outs[0].at[:, column]))
    return pairs


def id_row(ref, start, lanes):
    return ref[start : start + 16, lanes].astype(jnp.float32)[0:1, :]


def attend_kernel(cross, parts, asks, has_carry, final, partner, *refs):
    refs = list(refs)
    q_refs = [refs.pop(0) for _ in range(asks)]
    id_ref = refs.pop(0) if cross else None
    key_refs = [refs.pop(0) for _ in parts]
    carry_refs = [refs.pop(0) if has_carry else None for _ in range(asks)]
    other_ref = refs.pop(0) if partner else None
    out_refs = refs
    keys, values, key_ids = [], [], []
    for ref, (start, count) in zip(key_refs, parts, strict=True):
        if cross:
            for i in range(count):
                keys.append(ref[i, 0:X_V, :])
                values.append(ref[i, X_V:X_ID, :])
                key_ids += [id_row(ref.at[i], X_ID, slice(j, j + 128)) for j in (0, 128)]
            continue
        for i in range(start, start + count):
            keys.append(ref[i, 0:HALF, :])
            values.append(ref[i, ROW_V : ROW_V + HALF, :])
            key_ids.append(id_row(ref.at[i], ROW_ID, slice(0, 128)))
    keys = jnp.concatenate(keys, axis=0)
    values = jnp.concatenate(values, axis=0)
    q_row = 0 if cross else ROW_Q - ROW_ID
    def step(ask, block):
        q_ref, carry_ref, out_ref = q_refs[ask], carry_refs[ask], out_refs[ask]
        rows = rows_at(block, 256, 256)
        chunk = 2 * block
        query = q_ref[pl.ds(chunk, 2), q_row : q_row + HALF, :].reshape(256, HEAD_DIM)
        query = query * jnp.bfloat16(HEAD_DIM**-0.5)
        query_ids = []
        for i in (chunk, chunk + 1):
            row = id_ref.at[i][0:1, :] if cross else id_row(q_ref.at[i], 0, slice(0, 128))
            query_ids.append(jnp.transpose(jnp.broadcast_to(row, (128, 128))))
        query_ids = jnp.concatenate(query_ids, axis=0)
        match = jnp.concatenate([query_ids == ids for ids in key_ids], axis=1)
        scores = lax.dot_general(
            query, keys, (((1,), (1,)), ((), ())), preferred_element_type=jnp.float32
        )
        scores = jnp.where(match, scores, NEG)
        top = jnp.max(scores, axis=1, keepdims=True)
        if has_carry:
            old = carry_ref[rows, HEAD_DIM : HEAD_DIM + 1]
            top = jnp.maximum(top, old)
        else:
            top = jnp.maximum(top, LOW)
        weights = jnp.exp(scores - top)
        total = jnp.sum(weights, axis=1, keepdims=True)
        summed = jnp.dot(
            weights.astype(jnp.bfloat16), values, preferred_element_type=jnp.float32
        )
        if has_carry:
            scale = jnp.exp(old - top)
            total = total + scale * carry_ref[rows, HEAD_DIM + 64 : HEAD_DIM + 65]
            summed = summed + scale * carry_ref[rows, 0:HEAD_DIM]
        lane = lax.broadcasted_iota(jnp.int32, (256, 128), 1)
        if not final:
            out_ref[rows, 0:HEAD_DIM] = summed
            out_ref[rows, HEAD_DIM:WIDE] = jnp.where(lane < 64, top, total)
            return
        some = total > 0.0
        safe = jnp.where(some, total, 1.0)
        level = jnp.where(some, top + jnp.log(safe), NEG)
        summed = summed * (1.0 / safe)
        if partner:
            theirs_out = other_ref[pl.ds(chunk, 2)].reshape(256, WIDE)
            other = level_of(theirs_out[:, HEAD_DIM:WIDE])
            both = jnp.maximum(level, other)
            mine, theirs = jnp.exp(level - both), jnp.exp(other - both)
            share = 1.0 / (mine + theirs)
            summed = (mine * share) * summed + (theirs * share) * theirs_out[:, 0:HEAD_DIM].astype(jnp.float32)
            out_ref[rows, :] = summed.astype(jnp.bfloat16)
        else:
            high = level.astype(jnp.bfloat16).astype(jnp.float32)
            middle = (level - high).astype(jnp.bfloat16).astype(jnp.float32)
            low = level - high - middle
            three = jnp.where(lane < 32, high, jnp.where(lane < 64, middle, low))
            for half in (0, 1):
                pick = slice(half * HALF, half * HALF + HALF)
                out_ref[chunk + half, :, 0:HEAD_DIM] = summed[pick].astype(jnp.bfloat16)
                out_ref[chunk + half, :, HEAD_DIM:WIDE] = three[pick].astype(jnp.bfloat16)

    each = 2

    def body(i, _):
        for ask in range(asks):
            for sub in range(each):
                step(ask, each * i + sub)
        return 0

    lax.fori_loop(0, 4 // each, body, 0)


def level_of(lanes):
    lanes = lanes.astype(jnp.float32)
    return (lanes[:, 0:1] + lanes[:, 32:33]) + lanes[:, 64:65]


def attend(queries, keys, ids=None, carry=(), final=False, other=None):
    arrays = [array for array, _, _ in keys]
    operands = [*queries] + ([] if ids is None else [ids]) + arrays + [*carry]
    operands += [] if other is None else [other]
    aliases = {}
    if carry and not final:
        aliases = {len(queries) + len(keys) + i: i for i in range(len(queries))}
    if not final:
        out = jax.ShapeDtypeStruct((1024, WIDE), jnp.float32)
    elif other is None:
        out = shaped(8, HALF, WIDE)
    else:
        out = shaped(1024, HEAD_DIM)
    parts = tuple((start, count) for _, start, count in keys)
    width = sum(count for _, count in parts) * HALF * (1 if ids is None else 2)
    return pl.pallas_call(
        functools.partial(
            attend_kernel, ids is not None, parts, len(queries), len(carry) > 0, final, other is not None
        ),
        out_shape=[out] * len(queries),
        in_specs=[whole()] * len(operands),
        out_specs=[whole()] * len(queries),
        input_output_aliases=aliases,
        **params(4 * 1024 * len(queries) * width * HEAD_DIM, 4 * MIB, 10),
    )(*operands)


def merge_kernel(part_ref, out_ref):
    levels = [level_of(part_ref[i, :, HEAD_DIM:WIDE]) for i in range(8)]
    top = functools.reduce(jnp.maximum, levels)
    shares = [jnp.exp(level - top) for level in levels]
    summed = sum(
        share * part_ref[i, :, 0:HEAD_DIM].astype(jnp.float32) for i, share in enumerate(shares)
    )
    out_ref[...] = (summed * (1.0 / sum(shares))).astype(jnp.bfloat16)


def merge(part):
    return pl.pallas_call(
        merge_kernel,
        out_shape=shaped(HALF, HEAD_DIM),
        in_specs=[whole()],
        out_specs=whole(),
        **params(0, 2 * MIB),
    )(part)


def per_device(
    enc_query,
    enc_key,
    enc_value,
    input_segments,
    doc_bounds,
    target_query,
    cross_key,
    cross_value,
    target_segments,
):
    del doc_bounds
    ix, iz, ic = lax.axis_index("x"), lax.axis_index("z"), lax.axis_index("core")
    place = jnp.stack([iz, ic, ix]).astype(jnp.int32)
    local = functools.partial(copies, place)
    numbers = input_segments.reshape(2, HALF)
    target_ids = target_segments.reshape(4, 8, TGT).transpose(1, 0, 2).astype(jnp.float32)
    target_ids = jnp.broadcast_to(target_ids.reshape(8, 1, 128), (8, 8, 128))

    near, away, heads = load(
        place, enc_key, enc_value, enc_query, target_query, cross_key, cross_value, numbers
    )
    swapped = core_swap(away)
    def packed(shifts, after=()):
        plan = functools.partial(plan_pack, shifts)
        return local(plan, [near, swapped, numbers], [(ROWS, HEAD_DIM)] * len(shifts), after)

    sent = packed(ORDER[:5])
    got = [sent[0]] + [z_send(sent[k], ORDER[k]) for k in range(1, 5)]
    cross = lax.all_to_all(heads, "x", 0, 0, tiled=True)
    group, ask = local(plan_first, got, [(5, KEYS, HEAD_DIM), (5, ASK, HEAD_DIM)], [cross])


    sent = packed(ORDER[5:], [group])
    rest = [z_send(chunk, d) for chunk, d in zip(sent, ORDER[5:], strict=True)]
    left, right = x_send(group, 1), x_send(group, 3)
    to_right, to_left, mine = local(
        plan_second,
        [*rest, left, right, ask],
        [(6, KEYS, HEAD_DIM), (5, KEYS, HEAD_DIM), (8, ASK, HEAD_DIM)],
    )

    from_left, from_right = x_send(to_right, 1), x_send(to_left, 3)
    theirs = core_swap(mine)
    (targets,) = local(plan_targets, [cross], [(8, HALF, HEAD_DIM)], [to_right])
    targets = lax.all_to_all(targets, "z", 0, 0, tiled=True)
    queries = (mine, theirs)
    carry = attend(queries, [(group, 0, 5), (to_right, 3, 3)])
    carry = attend(queries, [(left, 0, 5), (right, 0, 5)], carry=carry)
    lasts = local(
        plan_third, [from_left, from_right], [(1, KEYS, HEAD_DIM), (2, KEYS, HEAD_DIM)], [carry[0], targets]
    )

    far = [x_send(lasts[0], 1), x_send(lasts[1], 3)]
    (part,) = attend([targets], [(cross, 0, 4)], ids=target_ids, final=True)
    part = lax.all_to_all(part, "z", 0, 0, tiled=True)
    carry = attend(queries, [(from_left, 0, 6), (from_right, 0, 5)], carry=carry)
    far_keys = [(far[0], 0, 1), (far[1], 0, 2)]
    (partial,) = attend([theirs], far_keys, carry=carry[1:], final=True)
    (done,) = attend([mine], far_keys, carry=carry[:1], final=True, other=core_swap(partial))

    (back,) = local(plan_back, [done], [(8, HALF, HEAD_DIM)])
    merged = merge(part)
    blocks = local(plan_cross_back, [merged], [(TGT, HEAD_DIM)] * 4, [back])
    blocks = [x_send(b, -d) if d else b for b, d in zip(blocks, X_ORDER, strict=True)]
    back = lax.all_to_all(back, "z", 0, 0, tiled=True)
    (away,) = local(plan_back_swap, [back], [(4, HALF, HEAD_DIM)], blocks)
    (enc_out,) = local(plan_unpack, [back, core_swap(away)], [(2 * HALF, 4 * HEAD_DIM)])
    (cross_out,) = local(plan_cross_unpack, blocks, [(TGT, 4 * HEAD_DIM)])
    return enc_out, cross_out


def solution(mesh):
    shape = mesh.shape
    split = Mesh(
        mesh.devices.reshape(4, shape["ctx"] // 4, shape["head"], shape["dp"]), ("x", "z", "core", "dp")
    )
    tokens = P(("dp", "x", "z"), "core")
    placed = (
        tokens,
        tokens,
        tokens,
        P(("dp", "x", "z")),
        P(("dp", "x", "z"), None),
        tokens,
        tokens,
        tokens,
        P("dp"),
    )
    return jax.shard_map(
        per_device, mesh=split, in_specs=placed, out_specs=(tokens, tokens), check_vma=False
    )
```

```python
import functools

import jax
import jax.numpy as jnp
from jax import lax
from jax.experimental import pallas as pl
from jax.experimental.pallas import tpu as pltpu
from jax.sharding import Mesh
from jax.sharding import PartitionSpec as P

HEAD_DIM = 256
HALF = 128
TGT = 32
NEG = -1.0e30
LOW = -1.0e29

ROW_V = HALF
ROW_ID = 2 * HALF
ROW_Q = ROW_ID + 16
ROWS = ROW_Q + HALF
KEYS = ROW_Q
ASK = ROWS - ROW_ID
X_V = 2 * HALF
X_ID = 4 * HALF
X_T = X_ID + 16
X_ROWS = X_T + 8 * TGT
ORDER = (0, 3, 5, 1, 7, 2, 6, 4)
X_ORDER = (0, 1, 3, 2)
WIDE = HEAD_DIM + 128
MIB = 1024 * 1024
HALF_TYPE = jnp.bfloat16


def z_send(array, shift):
    return lax.ppermute(array, "z", [(i, (i + shift) % 8) for i in range(8)])


def x_send(array, shift):
    return lax.ppermute(array, "x", [(i, (i + shift) % 4) for i in range(4)])


def core_swap(array):
    return lax.ppermute(array, "core", [(0, 1), (1, 0)])


def params(flops, moved, limit=8):
    return dict(
        compiler_params=pltpu.CompilerParams(vmem_limit_bytes=limit * MIB),
        cost_estimate=pl.CostEstimate(flops=flops, bytes_accessed=moved, transcendentals=0),
    )


def rows_at(start, size, unit):
    return pl.ds(pl.multiple_of(start * unit, unit), size)


def half_rows(c):
    return rows_at(c, HALF, HALF)


def columns(j):
    return pl.ds(j * HEAD_DIM, HEAD_DIM)


def whole():
    return pl.BlockSpec(memory_space=pltpu.VMEM)


def scalars():
    return pl.BlockSpec(memory_space=pltpu.SMEM)


def shaped(*shape):
    return jax.ShapeDtypeStruct(shape, HALF_TYPE)


def copy(a, b):
    b[...] = a[...]


def copies(place, plan, ins, outs, after=()):
    def kernel(place_ref, *refs):
        at = (place_ref[0], place_ref[1], place_ref[2])
        for a, b, *when in plan(at, refs[: len(ins)], refs[len(ins) + len(after) :]):
            if when:
                pl.when(when[0])(functools.partial(copy, a, b))
            else:
                copy(a, b)

    return pl.pallas_call(
        kernel,
        out_shape=[shaped(*shape) for shape in outs],
        in_specs=[scalars()] + [whole()] * len(ins) + [pl.BlockSpec(memory_space=pl.ANY)] * len(after),
        out_specs=[whole()] * len(outs),
        **params(0, 2 * MIB),
    )(place, *ins, *after)


def named(number_ref, half):
    row = number_ref[pl.ds(half, 1), :].astype(jnp.float32)
    return jnp.broadcast_to(row, (16, HALF)).astype(HALF_TYPE)


def run(made, sems):
    made = [pltpu.make_async_copy(a, b, sems.at[i]) for i, (a, b) in enumerate(made)]
    for one in made:
        one.start()
    return made


def load(place, keys, values, query):
    def kernel(place_ref, k_ref, v_ref, q_ref, near, away, sems):
        c = place_ref[1]
        made = []
        for side, out in ((1 - c, away), (c, near)):
            for i, ref in enumerate((k_ref, v_ref, q_ref)):
                made.append((ref.at[half_rows(side)], out.at[pl.ds(i * HALF, HALF)]))
        for one in run(made, sems):
            one.wait()

    return pl.pallas_call(
        kernel,
        out_shape=[shaped(3 * HALF, 4 * HEAD_DIM)] * 2,
        in_specs=[scalars()] + [pl.BlockSpec(memory_space=pl.ANY)] * 3,
        out_specs=[whole()] * 2,
        scratch_shapes=[pltpu.SemaphoreType.DMA((6,))],
        **params(0, 6 * MIB, 56),
    )(place, keys, values, query)


def load_cross(cross_keys, cross_values, numbers, targets, after):
    def kernel(xk_ref, xv_ref, id_ref, t_ref, _, heads, sems):
        made = []
        for j in range(4):
            for ref, row in ((xk_ref, 0), (xv_ref, X_V)):
                made.append((ref.at[:, columns(j)], heads.at[j, pl.ds(row, 2 * HALF)]))
            for z in range(8):
                made.append((t_ref.at[z, :, columns(j)], heads.at[j, pl.ds(X_T + z * TGT, TGT)]))
        made = run(made, sems)
        for j in range(4):
            for half in (0, 1):
                heads[j, X_ID:X_T, half * HALF : half * HALF + HALF] = named(id_ref, half)
        for one in made:
            one.wait()

    anywhere = pl.BlockSpec(memory_space=pl.ANY)
    return pl.pallas_call(
        kernel,
        out_shape=shaped(4, X_ROWS, HEAD_DIM),
        in_specs=[anywhere, anywhere, whole(), anywhere, anywhere],
        out_specs=whole(),
        scratch_shapes=[pltpu.SemaphoreType.DMA((40,))],
        **params(0, 4 * MIB, 56),
    )(cross_keys, cross_values, numbers, targets, after)


class Either:
    def __init__(self, first, a, b):
        self.first, self.a, self.b = first, a, b

    def __getitem__(self, key):
        return jnp.where(self.first, self.a[key], self.b[key])


class Row:
    def __init__(self, ref, half):
        self.ref, self.half = ref, half

    def __getitem__(self, key):
        row = named(self.ref, self.half)
        return jnp.concatenate([row, row], axis=1)


def plan_pack(shifts, at, ins, outs):
    z, c, _ = at
    near, swapped, ids = ins
    pairs = []
    for k, d in enumerate(shifts):
        head = lax.rem(z + d, 8)
        column = rows_at(lax.rem(head, 4), HEAD_DIM, HEAD_DIM)
        first = (head // 4) == c
        for i, row in enumerate((0, ROW_V, ROW_Q)):
            part = (pl.ds(i * HALF, HALF), column)
            pairs.append((Either(first, near.at[part], swapped.at[part]), outs[k].at[pl.ds(row, HALF)]))
        pairs.append((Row(ids, c), outs[k].at[pl.ds(ROW_ID, 16)]))
    return pairs


def plan_first(at, ins, outs):
    group, ask = outs
    pairs = []
    for i, ref in enumerate(ins):
        pairs.append((ref.at[pl.ds(0, KEYS)], group.at[i]))
        pairs.append((ref.at[pl.ds(ROW_ID, ASK)], ask.at[i]))
    return pairs


def plan_second(at, ins, outs):
    chunks, (left, right, ask_first) = ins[:3], ins[3:]
    to_right, to_left, ask = outs
    pairs = [
        (left.at[pl.ds(0, 3)], to_right.at[pl.ds(0, 3)]),
        (right.at[pl.ds(3, 2)], to_left.at[pl.ds(0, 2)]),
        (ask_first, ask.at[pl.ds(0, 5)]),
    ]
    for i, ref in enumerate(chunks):
        pairs.append((ref.at[pl.ds(0, KEYS)], to_right.at[3 + i]))
        pairs.append((ref.at[pl.ds(0, KEYS)], to_left.at[2 + i]))
        pairs.append((ref.at[pl.ds(ROW_ID, ASK)], ask.at[5 + i]))
    return pairs


def plan_third(at, ins, outs):
    return [(ins[0].at[pl.ds(3, 1)], outs[0]), (ins[1].at[pl.ds(3, 2)], outs[1])]


def plan_targets(at, ins, outs):
    return [
        (ins[0].at[x, pl.ds(X_T + z * TGT, TGT)], outs[0].at[z, pl.ds(x * TGT, TGT)])
        for x in range(4)
        for z in range(8)
    ]


def plan_back(at, ins, outs):
    z = at[0]
    return [
        (ins[0].at[pl.ds(k * HALF, HALF)], outs[0].at[lax.rem(z + 8 - d, 8)]) for k, d in enumerate(ORDER)
    ]


def plan_cross_back(at, ins, outs):
    x = at[2]
    return [
        (ins[0].at[rows_at(lax.rem(x + 4 - d, 4), TGT, TGT)], out) for d, out in zip(X_ORDER, outs, strict=True)
    ]


def plan_back_swap(at, ins, outs):
    return [(ins[0].at[pl.ds(4 * (1 - at[1]), 4)], outs[0])]


def plan_unpack(at, ins, outs):
    c = at[1]
    pairs = []
    back, swapped = ins[:2]
    for j in range(4):
        pairs.append((back.at[4 * c + j], outs[0].at[half_rows(c), columns(j)]))
        pairs.append((swapped.at[j], outs[0].at[half_rows(1 - c), columns(j)]))
    return pairs


def plan_cross_unpack(at, ins, outs):
    pairs = []
    for piece, shift in zip(ins, X_ORDER, strict=True):
        column = rows_at(lax.rem(at[2] + shift, 4), HEAD_DIM, HEAD_DIM)
        pairs.append((piece, outs[0].at[:, column]))
    return pairs


def id_row(ref, start, lanes):
    return ref[start : start + 16, lanes].astype(jnp.float32)[0:1, :]


def attend_kernel(cross, parts, asks, has_carry, final, partner, *refs):
    refs = list(refs)
    q_refs = [refs.pop(0) for _ in range(asks)]
    id_ref = refs.pop(0) if cross else None
    key_refs = [refs.pop(0) for _ in parts]
    carry_refs = [refs.pop(0) if has_carry else None for _ in range(asks)]
    other_ref = refs.pop(0) if partner else None
    out_refs = refs
    keys, values, key_ids = [], [], []
    for ref, (start, count) in zip(key_refs, parts, strict=True):
        if cross:
            for i in range(count):
                keys.append(ref[i, 0:X_V, :])
                values.append(ref[i, X_V:X_ID, :])
                key_ids += [id_row(ref.at[i], X_ID, slice(j, j + 128)) for j in (0, 128)]
            continue
        for i in range(start, start + count):
            keys.append(ref[i, 0:HALF, :])
            values.append(ref[i, ROW_V : ROW_V + HALF, :])
            key_ids.append(id_row(ref.at[i], ROW_ID, slice(0, 128)))
    keys = jnp.concatenate(keys, axis=0)
    values = jnp.concatenate(values, axis=0)
    q_row = 0 if cross else ROW_Q - ROW_ID
    def step(ask, block):
        q_ref, carry_ref, out_ref = q_refs[ask], carry_refs[ask], out_refs[ask]
        rows = rows_at(block, 256, 256)
        chunk = 2 * block
        query = q_ref[pl.ds(chunk, 2), q_row : q_row + HALF, :].reshape(256, HEAD_DIM)
        query = query * jnp.bfloat16(HEAD_DIM**-0.5)
        query_ids = []
        for i in (chunk, chunk + 1):
            row = id_ref.at[i][0:1, :] if cross else id_row(q_ref.at[i], 0, slice(0, 128))
            query_ids.append(jnp.transpose(jnp.broadcast_to(row, (128, 128))))
        query_ids = jnp.concatenate(query_ids, axis=0)
        match = jnp.concatenate([query_ids == ids for ids in key_ids], axis=1)
        scores = lax.dot_general(
            query, keys, (((1,), (1,)), ((), ())), preferred_element_type=jnp.float32
        )
        scores = jnp.where(match, scores, NEG)
        top = jnp.max(scores, axis=1, keepdims=True)
        if has_carry:
            old = carry_ref[rows, HEAD_DIM : HEAD_DIM + 1]
            top = jnp.maximum(top, old)
        else:
            top = jnp.maximum(top, LOW)
        weights = jnp.exp(scores - top)
        total = jnp.sum(weights, axis=1, keepdims=True)
        summed = jnp.dot(
            weights.astype(jnp.bfloat16), values, preferred_element_type=jnp.float32
        )
        if has_carry:
            scale = jnp.exp(old - top)
            total = total + scale * carry_ref[rows, HEAD_DIM + 64 : HEAD_DIM + 65]
            summed = summed + scale * carry_ref[rows, 0:HEAD_DIM]
        lane = lax.broadcasted_iota(jnp.int32, (256, 128), 1)
        if not final:
            out_ref[rows, 0:HEAD_DIM] = summed
            out_ref[rows, HEAD_DIM:WIDE] = jnp.where(lane < 64, top, total)
            return
        some = total > 0.0
        safe = jnp.where(some, total, 1.0)
        level = jnp.where(some, top + jnp.log(safe), NEG)
        summed = summed * (1.0 / safe)
        if partner:
            theirs_out = other_ref[pl.ds(chunk, 2)].reshape(256, WIDE)
            other = level_of(theirs_out[:, HEAD_DIM:WIDE])
            both = jnp.maximum(level, other)
            mine, theirs = jnp.exp(level - both), jnp.exp(other - both)
            share = 1.0 / (mine + theirs)
            summed = (mine * share) * summed + (theirs * share) * theirs_out[:, 0:HEAD_DIM].astype(jnp.float32)
            out_ref[rows, :] = summed.astype(jnp.bfloat16)
        else:
            high = level.astype(jnp.bfloat16).astype(jnp.float32)
            middle = (level - high).astype(jnp.bfloat16).astype(jnp.float32)
            low = level - high - middle
            three = jnp.where(lane < 32, high, jnp.where(lane < 64, middle, low))
            for half in (0, 1):
                pick = slice(half * HALF, half * HALF + HALF)
                out_ref[chunk + half, :, 0:HEAD_DIM] = summed[pick].astype(jnp.bfloat16)
                out_ref[chunk + half, :, HEAD_DIM:WIDE] = three[pick].astype(jnp.bfloat16)

    each = 2

    def body(i, _):
        for ask in range(asks):
            for sub in range(each):
                step(ask, each * i + sub)
        return 0

    lax.fori_loop(0, 4 // each, body, 0)


def level_of(lanes):
    lanes = lanes.astype(jnp.float32)
    return (lanes[:, 0:1] + lanes[:, 32:33]) + lanes[:, 64:65]


def attend(queries, keys, ids=None, carry=(), final=False, other=None):
    arrays = [array for array, _, _ in keys]
    operands = [*queries] + ([] if ids is None else [ids]) + arrays + [*carry]
    operands += [] if other is None else [other]
    aliases = {}
    if carry and not final:
        aliases = {len(queries) + len(keys) + i: i for i in range(len(queries))}
    if not final:
        out = jax.ShapeDtypeStruct((1024, WIDE), jnp.float32)
    elif other is None:
        out = shaped(8, HALF, WIDE)
    else:
        out = shaped(1024, HEAD_DIM)
    parts = tuple((start, count) for _, start, count in keys)
    width = sum(count for _, count in parts) * HALF * (1 if ids is None else 2)
    return pl.pallas_call(
        functools.partial(
            attend_kernel, ids is not None, parts, len(queries), len(carry) > 0, final, other is not None
        ),
        out_shape=[out] * len(queries),
        in_specs=[whole()] * len(operands),
        out_specs=[whole()] * len(queries),
        input_output_aliases=aliases,
        **params(4 * 1024 * len(queries) * width * HEAD_DIM, 4 * MIB, 24),
    )(*operands)


def merge_kernel(part_ref, out_ref):
    levels = [level_of(part_ref[i, :, HEAD_DIM:WIDE]) for i in range(8)]
    top = functools.reduce(jnp.maximum, levels)
    shares = [jnp.exp(level - top) for level in levels]
    summed = sum(
        share * part_ref[i, :, 0:HEAD_DIM].astype(jnp.float32) for i, share in enumerate(shares)
    )
    out_ref[...] = (summed * (1.0 / sum(shares))).astype(jnp.bfloat16)


def merge(part):
    return pl.pallas_call(
        merge_kernel,
        out_shape=shaped(HALF, HEAD_DIM),
        in_specs=[whole()],
        out_specs=whole(),
        **params(0, 2 * MIB),
    )(part)


def per_device(
    enc_query,
    enc_key,
    enc_value,
    input_segments,
    doc_bounds,
    target_query,
    cross_key,
    cross_value,
    target_segments,
):
    del doc_bounds
    ix, iz, ic = lax.axis_index("x"), lax.axis_index("z"), lax.axis_index("core")
    place = jnp.stack([iz, ic, ix]).astype(jnp.int32)
    local = functools.partial(copies, place)
    numbers = input_segments.reshape(2, HALF)
    target_ids = target_segments.reshape(4, 8, TGT).transpose(1, 0, 2).astype(jnp.float32)
    target_ids = jnp.broadcast_to(target_ids.reshape(8, 1, 128), (8, 8, 128))

    spread = jnp.broadcast_to(target_query[None], (8, TGT, 4 * HEAD_DIM))
    spread = lax.all_to_all(spread, "z", 0, 0, tiled=True)
    near, away = load(place, enc_key, enc_value, enc_query)
    swapped = core_swap(away)
    def packed(shifts, after=()):
        plan = functools.partial(plan_pack, shifts)
        return local(plan, [near, swapped, numbers], [(ROWS, HEAD_DIM)] * len(shifts), after)

    sent = packed(ORDER[:5])
    got = [sent[0]] + [z_send(sent[k], ORDER[k]) for k in range(1, 5)]
    heads = load_cross(cross_key, cross_value, numbers, spread, got[3])
    cross = lax.all_to_all(heads, "x", 0, 0, tiled=True)
    group, ask = local(plan_first, got, [(5, KEYS, HEAD_DIM), (5, ASK, HEAD_DIM)], [heads])


    sent = packed(ORDER[5:], [group])
    rest = [z_send(chunk, d) for chunk, d in zip(sent, ORDER[5:], strict=True)]
    left, right = x_send(group, 1), x_send(group, 3)
    to_right, to_left, mine = local(
        plan_second,
        [*rest, left, right, ask],
        [(6, KEYS, HEAD_DIM), (5, KEYS, HEAD_DIM), (8, ASK, HEAD_DIM)],
    )

    from_left, from_right = x_send(to_right, 1), x_send(to_left, 3)
    theirs = core_swap(mine)
    (targets,) = local(plan_targets, [cross], [(8, HALF, HEAD_DIM)], [to_right])
    (part,) = attend([targets], [(cross, 0, 4)], ids=target_ids, final=True)
    part = lax.all_to_all(part, "z", 0, 0, tiled=True)
    queries = (mine, theirs)
    carry = attend(queries, [(group, 0, 5), (to_right, 3, 3), (left, 0, 5), (right, 0, 5)])
    lasts = local(
        plan_third, [from_left, from_right], [(1, KEYS, HEAD_DIM), (2, KEYS, HEAD_DIM)], [carry[0]]
    )

    far = [x_send(lasts[0], 1), x_send(lasts[1], 3)]
    carry = attend(queries, [(from_left, 0, 6), (from_right, 0, 5)], carry=carry)
    far_keys = [(far[0], 0, 1), (far[1], 0, 2)]
    (partial,) = attend([theirs], far_keys, carry=carry[1:], final=True)
    (done,) = attend([mine], far_keys, carry=carry[:1], final=True, other=core_swap(partial))

    (back,) = local(plan_back, [done], [(8, HALF, HEAD_DIM)])
    merged = merge(part)
    blocks = local(plan_cross_back, [merged], [(TGT, HEAD_DIM)] * 4, [back])
    blocks = [x_send(b, -d) if d else b for b, d in zip(blocks, X_ORDER, strict=True)]
    back = lax.all_to_all(back, "z", 0, 0, tiled=True)
    (away,) = local(plan_back_swap, [back], [(4, HALF, HEAD_DIM)], blocks)
    (enc_out,) = local(plan_unpack, [back, core_swap(away)], [(2 * HALF, 4 * HEAD_DIM)])
    (cross_out,) = local(plan_cross_unpack, blocks, [(TGT, 4 * HEAD_DIM)])
    return enc_out, cross_out


def solution(mesh):
    shape = mesh.shape
    split = Mesh(
        mesh.devices.reshape(4, shape["ctx"] // 4, shape["head"], shape["dp"]), ("x", "z", "core", "dp")
    )
    tokens = P(("dp", "x", "z"), "core")
    placed = (
        tokens,
        tokens,
        tokens,
        P(("dp", "x", "z")),
        P(("dp", "x", "z"), None),
        tokens,
        tokens,
        tokens,
        P("dp"),
    )
    return jax.shard_map(
        per_device, mesh=split, in_specs=placed, out_specs=(tokens, tokens), check_vma=False
    )
```

```python
import functools

import jax
import jax.numpy as jnp
from jax import lax
from jax.experimental import pallas as pl
from jax.experimental.pallas import tpu as pltpu
from jax.sharding import Mesh
from jax.sharding import PartitionSpec as P

HEAD_DIM = 256
HALF = 128
TGT = 32
NEG = -1.0e30
LOW = -1.0e29

ROW_V = HALF
ROW_ID = 2 * HALF
ROW_Q = ROW_ID + 16
ROWS = ROW_Q + HALF
KEYS = ROW_Q
ASK = ROWS - ROW_ID
X_V = 2 * HALF
X_ID = 4 * HALF
X_T = X_ID + 16
X_ROWS = X_T + 8 * TGT
ORDER = (0, 3, 5, 1, 7, 2, 6, 4)
X_ORDER = (0, 1, 3, 2)
WIDE = HEAD_DIM + 128
MIB = 1024 * 1024
HALF_TYPE = jnp.bfloat16


def z_send(array, shift):
    return lax.ppermute(array, "z", [(i, (i + shift) % 8) for i in range(8)])


def x_send(array, shift):
    return lax.ppermute(array, "x", [(i, (i + shift) % 4) for i in range(4)])


def core_swap(array):
    return lax.ppermute(array, "core", [(0, 1), (1, 0)])


def params(flops, moved, limit=8):
    return dict(
        compiler_params=pltpu.CompilerParams(vmem_limit_bytes=limit * MIB),
        cost_estimate=pl.CostEstimate(flops=flops, bytes_accessed=moved, transcendentals=0),
    )


def rows_at(start, size, unit):
    if isinstance(start, int):
        return pl.ds(start * unit, size)
    return pl.ds(pl.multiple_of(start * unit, unit), size)


def half_rows(c):
    return rows_at(c, HALF, HALF)


def columns(j):
    return pl.ds(j * HEAD_DIM, HEAD_DIM)


def whole():
    return pl.BlockSpec(memory_space=pltpu.VMEM)


def scalars():
    return pl.BlockSpec(memory_space=pltpu.SMEM)


def shaped(*shape):
    return jax.ShapeDtypeStruct(shape, HALF_TYPE)


def copy(a, b):
    b[...] = a[...]


def copies(place, plan, ins, outs, after=()):
    def kernel(place_ref, *refs):
        at = (place_ref[0], place_ref[1], place_ref[2])
        for a, b, *when in plan(at, refs[: len(ins)], refs[len(ins) + len(after) :]):
            if when:
                pl.when(when[0])(functools.partial(copy, a, b))
            else:
                copy(a, b)

    return pl.pallas_call(
        kernel,
        out_shape=[shaped(*shape) for shape in outs],
        in_specs=[scalars()] + [whole()] * len(ins) + [pl.BlockSpec(memory_space=pl.ANY)] * len(after),
        out_specs=[whole()] * len(outs),
        **params(0, 2 * MIB),
    )(place, *ins, *after)


def named(number_ref, half):
    row = number_ref[pl.ds(half, 1), :].astype(jnp.float32)
    return jnp.broadcast_to(row, (16, HALF)).astype(HALF_TYPE)


def run(made, sems):
    made = [pltpu.make_async_copy(a, b, sems.at[i]) for i, (a, b) in enumerate(made)]
    for one in made:
        one.start()
    return made


def load(place, keys, values, query):
    def kernel(place_ref, k_ref, v_ref, q_ref, near, away, sems):
        c = place_ref[1]
        made = []
        for side, out in ((1 - c, away), (c, near)):
            for i, ref in enumerate((k_ref, v_ref, q_ref)):
                made.append((ref.at[half_rows(side)], out.at[pl.ds(i * HALF, HALF)]))
        for one in run(made, sems):
            one.wait()

    return pl.pallas_call(
        kernel,
        out_shape=[shaped(3 * HALF, 4 * HEAD_DIM)] * 2,
        in_specs=[scalars()] + [pl.BlockSpec(memory_space=pl.ANY)] * 3,
        out_specs=[whole()] * 2,
        scratch_shapes=[pltpu.SemaphoreType.DMA((6,))],
        **params(0, 6 * MIB, 56),
    )(place, keys, values, query)


def load_cross(cross_keys, cross_values, numbers, targets, after):
    def kernel(xk_ref, xv_ref, id_ref, t_ref, _, heads, sems):
        made = []
        for j in range(4):
            for ref, row in ((xk_ref, 0), (xv_ref, X_V)):
                made.append((ref.at[:, columns(j)], heads.at[j, pl.ds(row, 2 * HALF)]))
            for z in range(8):
                made.append((t_ref.at[z, :, columns(j)], heads.at[j, pl.ds(X_T + z * TGT, TGT)]))
        made = run(made, sems)
        for j in range(4):
            for half in (0, 1):
                heads[j, X_ID:X_T, half * HALF : half * HALF + HALF] = named(id_ref, half)
        for one in made:
            one.wait()

    anywhere = pl.BlockSpec(memory_space=pl.ANY)
    return pl.pallas_call(
        kernel,
        out_shape=shaped(4, X_ROWS, HEAD_DIM),
        in_specs=[anywhere, anywhere, whole(), anywhere, anywhere],
        out_specs=whole(),
        scratch_shapes=[pltpu.SemaphoreType.DMA((40,))],
        **params(0, 4 * MIB, 56),
    )(cross_keys, cross_values, numbers, targets, after)


class Either:
    def __init__(self, first, a, b):
        self.first, self.a, self.b = first, a, b

    def __getitem__(self, key):
        return jnp.where(self.first, self.a[key], self.b[key])


class Row:
    def __init__(self, ref, half):
        self.ref, self.half = ref, half

    def __getitem__(self, key):
        row = named(self.ref, self.half)
        return jnp.concatenate([row, row], axis=1)


def plan_pack(shifts, at, ins, outs):
    z, c, _ = at
    near, swapped, ids = ins
    pairs = []
    for k, d in enumerate(shifts):
        head = lax.rem(z + d, 8)
        column = rows_at(lax.rem(head, 4), HEAD_DIM, HEAD_DIM)
        first = (head // 4) == c
        for i, row in enumerate((0, ROW_V, ROW_Q)):
            part = (pl.ds(i * HALF, HALF), column)
            pairs.append((Either(first, near.at[part], swapped.at[part]), outs[k].at[pl.ds(row, HALF)]))
        pairs.append((Row(ids, c), outs[k].at[pl.ds(ROW_ID, 16)]))
    return pairs


def plan_first(at, ins, outs):
    group, ask = outs
    pairs = []
    for i, ref in enumerate(ins):
        pairs.append((ref.at[pl.ds(0, KEYS)], group.at[i]))
        pairs.append((ref.at[pl.ds(ROW_ID, ASK)], ask.at[i]))
    return pairs


def plan_second(at, ins, outs):
    chunks, (left, right, ask_first) = ins[:3], ins[3:]
    to_right, to_left, ask = outs
    pairs = [
        (left.at[pl.ds(0, 3)], to_right.at[pl.ds(0, 3)]),
        (right.at[pl.ds(3, 2)], to_left.at[pl.ds(0, 2)]),
        (ask_first, ask.at[pl.ds(0, 5)]),
    ]
    for i, ref in enumerate(chunks):
        pairs.append((ref.at[pl.ds(0, KEYS)], to_right.at[3 + i]))
        pairs.append((ref.at[pl.ds(0, KEYS)], to_left.at[2 + i]))
        pairs.append((ref.at[pl.ds(ROW_ID, ASK)], ask.at[5 + i]))
    return pairs


def plan_third(at, ins, outs):
    return [(ins[0].at[pl.ds(3, 1)], outs[0]), (ins[1].at[pl.ds(3, 2)], outs[1])]


def plan_targets(at, ins, outs):
    return [
        (ins[0].at[x, pl.ds(X_T + z * TGT, TGT)], outs[0].at[z, pl.ds(x * TGT, TGT)])
        for x in range(4)
        for z in range(8)
    ]


def plan_cross_back(at, ins, outs):
    x = at[2]
    return [
        (ins[0].at[rows_at(lax.rem(x + 4 - d, 4), TGT, TGT)], out) for d, out in zip(X_ORDER, outs, strict=True)
    ]


def plan_back_swap(at, ins, outs):
    return [(ins[0].at[pl.ds(4 * (1 - at[1]), 4)], outs[0])]


def plan_unpack(at, ins, outs):
    c = at[1]
    pairs = []
    back, swapped = ins[:2]
    for j in range(4):
        pairs.append((back.at[4 * c + j], outs[0].at[half_rows(c), columns(j)]))
        pairs.append((swapped.at[j], outs[0].at[half_rows(1 - c), columns(j)]))
    return pairs


def plan_cross_unpack(at, ins, outs):
    pairs = []
    for piece, shift in zip(ins, X_ORDER, strict=True):
        column = rows_at(lax.rem(at[2] + shift, 4), HEAD_DIM, HEAD_DIM)
        pairs.append((piece, outs[0].at[:, column]))
    return pairs


def id_row(ref, start, lanes):
    return ref[start : start + 16, lanes].astype(jnp.float32)[0:1, :]


def attend_kernel(cross, parts, asks, has_carry, final, partner, *refs):
    refs = list(refs)
    place_ref = refs.pop(0) if partner else None
    q_refs = [refs.pop(0) for _ in range(asks)]
    id_ref = refs.pop(0) if cross else None
    key_refs = [refs.pop(0) for _ in parts]
    carry_refs = [refs.pop(0) if has_carry else None for _ in range(asks)]
    other_ref = refs.pop(0) if partner else None
    out_refs = refs
    keys, values, key_ids = [], [], []
    for ref, (start, count) in zip(key_refs, parts, strict=True):
        if cross:
            for i in range(count):
                keys.append(ref[i, 0:X_V, :])
                values.append(ref[i, X_V:X_ID, :])
                key_ids += [id_row(ref.at[i], X_ID, slice(j, j + 128)) for j in (0, 128)]
            continue
        for i in range(start, start + count):
            keys.append(ref[i, 0:HALF, :])
            values.append(ref[i, ROW_V : ROW_V + HALF, :])
            key_ids.append(id_row(ref.at[i], ROW_ID, slice(0, 128)))
    keys = jnp.concatenate(keys, axis=0)
    values = jnp.concatenate(values, axis=0)
    q_row = 0 if cross else ROW_Q - ROW_ID
    def step(ask, block):
        q_ref, carry_ref, out_ref = q_refs[ask], carry_refs[ask], out_refs[ask]
        rows = rows_at(block, 256, 256)
        chunk = 2 * block
        query = q_ref[pl.ds(chunk, 2), q_row : q_row + HALF, :].reshape(256, HEAD_DIM)
        query = query * jnp.bfloat16(HEAD_DIM**-0.5)
        query_ids = []
        for i in (chunk, chunk + 1):
            row = id_ref.at[i][0:1, :] if cross else id_row(q_ref.at[i], 0, slice(0, 128))
            query_ids.append(jnp.transpose(jnp.broadcast_to(row, (128, 128))))
        query_ids = jnp.concatenate(query_ids, axis=0)
        match = jnp.concatenate([query_ids == ids for ids in key_ids], axis=1)
        scores = lax.dot_general(
            query, keys, (((1,), (1,)), ((), ())), preferred_element_type=jnp.float32
        )
        scores = jnp.where(match, scores, NEG)
        top = jnp.max(scores, axis=1, keepdims=True)
        if has_carry:
            old = carry_ref[rows, HEAD_DIM : HEAD_DIM + 1]
            top = jnp.maximum(top, old)
        else:
            top = jnp.maximum(top, LOW)
        weights = jnp.exp(scores - top)
        total = jnp.sum(weights, axis=1, keepdims=True)
        summed = jnp.dot(
            weights.astype(jnp.bfloat16), values, preferred_element_type=jnp.float32
        )
        if has_carry:
            scale = jnp.exp(old - top)
            total = total + scale * carry_ref[rows, HEAD_DIM + 64 : HEAD_DIM + 65]
            summed = summed + scale * carry_ref[rows, 0:HEAD_DIM]
        lane = lax.broadcasted_iota(jnp.int32, (256, 128), 1)
        if not final:
            out_ref[rows, 0:HEAD_DIM] = summed
            out_ref[rows, HEAD_DIM:WIDE] = jnp.where(lane < 64, top, total)
            return
        some = total > 0.0
        safe = jnp.where(some, total, 1.0)
        level = jnp.where(some, top + jnp.log(safe), NEG)
        summed = summed * (1.0 / safe)
        if partner:
            theirs_out = other_ref[pl.ds(chunk, 2)].reshape(256, WIDE)
            other = level_of(theirs_out[:, HEAD_DIM:WIDE])
            both = jnp.maximum(level, other)
            mine, theirs = jnp.exp(level - both), jnp.exp(other - both)
            share = 1.0 / (mine + theirs)
            summed = (mine * share) * summed + (theirs * share) * theirs_out[:, 0:HEAD_DIM].astype(jnp.float32)
            for half in (0, 1):
                to = lax.rem(place_ref[0] + 8 - ORDER[chunk + half], 8)
                out_ref[to] = summed[half * HALF : half * HALF + HALF].astype(jnp.bfloat16)
        else:
            high = level.astype(jnp.bfloat16).astype(jnp.float32)
            middle = (level - high).astype(jnp.bfloat16).astype(jnp.float32)
            low = level - high - middle
            three = jnp.where(lane < 32, high, jnp.where(lane < 64, middle, low))
            for half in (0, 1):
                pick = slice(half * HALF, half * HALF + HALF)
                out_ref[chunk + half, :, 0:HEAD_DIM] = summed[pick].astype(jnp.bfloat16)
                out_ref[chunk + half, :, HEAD_DIM:WIDE] = three[pick].astype(jnp.bfloat16)

    each = 2

    def body(i, _):
        for ask in range(asks):
            for sub in range(each):
                step(ask, each * i + sub)
        return 0

    if partner:
        for block in range(4):
            step(0, block)
    else:
        lax.fori_loop(0, 4 // each, body, 0)


def level_of(lanes):
    lanes = lanes.astype(jnp.float32)
    return (lanes[:, 0:1] + lanes[:, 32:33]) + lanes[:, 64:65]


def attend(queries, keys, ids=None, carry=(), final=False, other=None, place=None):
    arrays = [array for array, _, _ in keys]
    operands = [*queries] + ([] if ids is None else [ids]) + arrays + [*carry]
    operands += [] if other is None else [other]
    aliases = {}
    if carry and not final:
        aliases = {len(queries) + len(keys) + i: i for i in range(len(queries))}
    if not final:
        out = jax.ShapeDtypeStruct((1024, WIDE), jnp.float32)
    elif other is None:
        out = shaped(8, HALF, WIDE)
    else:
        out = shaped(8, HALF, HEAD_DIM)
    parts = tuple((start, count) for _, start, count in keys)
    width = sum(count for _, count in parts) * HALF * (1 if ids is None else 2)
    specs = [whole()] * len(operands)
    if other is not None:
        operands, specs = [place] + operands, [scalars()] + specs
    return pl.pallas_call(
        functools.partial(
            attend_kernel, ids is not None, parts, len(queries), len(carry) > 0, final, other is not None
        ),
        out_shape=[out] * len(queries),
        in_specs=specs,
        out_specs=[whole()] * len(queries),
        input_output_aliases=aliases,
        **params(4 * 1024 * len(queries) * width * HEAD_DIM, 4 * MIB, 24),
    )(*operands)


def merge_kernel(part_ref, out_ref):
    levels = [level_of(part_ref[i, :, HEAD_DIM:WIDE]) for i in range(8)]
    top = functools.reduce(jnp.maximum, levels)
    shares = [jnp.exp(level - top) for level in levels]
    summed = sum(
        share * part_ref[i, :, 0:HEAD_DIM].astype(jnp.float32) for i, share in enumerate(shares)
    )
    out_ref[...] = (summed * (1.0 / sum(shares))).astype(jnp.bfloat16)


def merge(part):
    return pl.pallas_call(
        merge_kernel,
        out_shape=shaped(HALF, HEAD_DIM),
        in_specs=[whole()],
        out_specs=whole(),
        **params(0, 2 * MIB),
    )(part)


def per_device(
    enc_query,
    enc_key,
    enc_value,
    input_segments,
    doc_bounds,
    target_query,
    cross_key,
    cross_value,
    target_segments,
):
    del doc_bounds
    ix, iz, ic = lax.axis_index("x"), lax.axis_index("z"), lax.axis_index("core")
    place = jnp.stack([iz, ic, ix]).astype(jnp.int32)
    local = functools.partial(copies, place)
    numbers = input_segments.reshape(2, HALF)
    target_ids = target_segments.reshape(4, 8, TGT).transpose(1, 0, 2).astype(jnp.float32)
    target_ids = jnp.broadcast_to(target_ids.reshape(8, 1, 128), (8, 8, 128))

    spread = jnp.broadcast_to(target_query[None], (8, TGT, 4 * HEAD_DIM))
    spread = lax.all_to_all(spread, "z", 0, 0, tiled=True)
    near, away = load(place, enc_key, enc_value, enc_query)
    swapped = core_swap(away)
    def packed(shifts, after=()):
        plan = functools.partial(plan_pack, shifts)
        return local(plan, [near, swapped, numbers], [(ROWS, HEAD_DIM)] * len(shifts), after)

    sent = packed(ORDER[:5])
    got = [sent[0]] + [z_send(sent[k], ORDER[k]) for k in range(1, 5)]
    heads = load_cross(cross_key, cross_value, numbers, spread, got[3])
    cross = lax.all_to_all(heads, "x", 0, 0, tiled=True)
    group, ask = local(plan_first, got, [(5, KEYS, HEAD_DIM), (5, ASK, HEAD_DIM)], [heads])


    sent = packed(ORDER[5:], [got[3]])
    rest = [z_send(chunk, d) for chunk, d in zip(sent, ORDER[5:], strict=True)]
    left, right = x_send(group, 1), x_send(group, 3)
    to_right, to_left, mine = local(
        plan_second,
        [*rest, left, right, ask],
        [(6, KEYS, HEAD_DIM), (5, KEYS, HEAD_DIM), (8, ASK, HEAD_DIM)],
    )

    from_left, from_right = x_send(to_right, 1), x_send(to_left, 3)
    theirs = core_swap(mine)
    (targets,) = local(plan_targets, [cross], [(8, HALF, HEAD_DIM)], [to_right])
    (part,) = attend([targets], [(cross, 0, 4)], ids=target_ids, final=True)
    part = lax.all_to_all(part, "z", 0, 0, tiled=True)
    queries = (mine, theirs)
    carry = attend(queries, [(group, 0, 5), (to_right, 3, 3), (left, 0, 5), (right, 0, 5)])
    lasts = local(
        plan_third, [from_left, from_right], [(1, KEYS, HEAD_DIM), (2, KEYS, HEAD_DIM)], [carry[0]]
    )

    far = [x_send(lasts[0], 1), x_send(lasts[1], 3)]
    carry = attend(queries, [(from_left, 0, 6), (from_right, 0, 5)], carry=carry)
    far_keys = [(far[0], 0, 1), (far[1], 0, 2)]
    (partial,) = attend([theirs], far_keys, carry=carry[1:], final=True)
    (back,) = attend([mine], far_keys, carry=carry[:1], final=True, other=core_swap(partial), place=place)

    merged = merge(part)
    blocks = local(plan_cross_back, [merged], [(TGT, HEAD_DIM)] * 4, [back])
    blocks = [x_send(b, -d) if d else b for b, d in zip(blocks, X_ORDER, strict=True)]
    back = lax.all_to_all(back, "z", 0, 0, tiled=True)
    (away,) = local(plan_back_swap, [back], [(4, HALF, HEAD_DIM)], blocks)
    (enc_out,) = local(plan_unpack, [back, core_swap(away)], [(2 * HALF, 4 * HEAD_DIM)])
    (cross_out,) = local(plan_cross_unpack, blocks, [(TGT, 4 * HEAD_DIM)])
    return enc_out, cross_out


def solution(mesh):
    shape = mesh.shape
    split = Mesh(
        mesh.devices.reshape(4, shape["ctx"] // 4, shape["head"], shape["dp"]), ("x", "z", "core", "dp")
    )
    tokens = P(("dp", "x", "z"), "core")
    placed = (
        tokens,
        tokens,
        tokens,
        P(("dp", "x", "z")),
        P(("dp", "x", "z"), None),
        tokens,
        tokens,
        tokens,
        P("dp"),
    )
    return jax.shard_map(
        per_device, mesh=split, in_specs=placed, out_specs=(tokens, tokens), check_vma=False
    )
```

```python
import functools

import jax
import jax.numpy as jnp
from jax import lax
from jax.experimental import pallas as pl
from jax.experimental.pallas import tpu as pltpu
from jax.sharding import Mesh
from jax.sharding import PartitionSpec as P

HEAD_DIM = 256
HALF = 128
TGT = 32
NEG = -1.0e30
LOW = -1.0e29

ROW_V = HALF
ROW_ID = 2 * HALF
ROW_Q = ROW_ID + 16
ROWS = ROW_Q + HALF
KEYS = ROW_Q
ASK = ROWS - ROW_ID
X_V = 2 * HALF
X_ID = 4 * HALF
X_T = X_ID + 16
X_ROWS = X_T + 8 * TGT
ORDER = (0, 3, 5, 1, 7, 2, 6, 4)
X_ORDER = (0, 1, 3, 2)
WIDE = HEAD_DIM + 128
MIB = 1024 * 1024
HALF_TYPE = jnp.bfloat16


def z_send(array, shift):
    return lax.ppermute(array, "z", [(i, (i + shift) % 8) for i in range(8)])


def x_send(array, shift):
    return lax.ppermute(array, "x", [(i, (i + shift) % 4) for i in range(4)])


def core_swap(array):
    return lax.ppermute(array, "core", [(0, 1), (1, 0)])


def params(flops, moved, limit=8):
    return dict(
        compiler_params=pltpu.CompilerParams(vmem_limit_bytes=limit * MIB),
        cost_estimate=pl.CostEstimate(flops=flops, bytes_accessed=moved, transcendentals=0),
    )


def rows_at(start, size, unit):
    if isinstance(start, int):
        return pl.ds(start * unit, size)
    return pl.ds(pl.multiple_of(start * unit, unit), size)


def half_rows(c):
    return rows_at(c, HALF, HALF)


def columns(j):
    return pl.ds(j * HEAD_DIM, HEAD_DIM)


def whole():
    return pl.BlockSpec(memory_space=pltpu.VMEM)


def scalars():
    return pl.BlockSpec(memory_space=pltpu.SMEM)


def shaped(*shape):
    return jax.ShapeDtypeStruct(shape, HALF_TYPE)


def copy(a, b):
    b[...] = a[...]


def copies(place, plan, ins, outs, after=()):
    def kernel(place_ref, *refs):
        at = (place_ref[0], place_ref[1], place_ref[2])
        for a, b, *when in plan(at, refs[: len(ins)], refs[len(ins) + len(after) :]):
            if when:
                pl.when(when[0])(functools.partial(copy, a, b))
            else:
                copy(a, b)

    return pl.pallas_call(
        kernel,
        out_shape=[shaped(*shape) for shape in outs],
        in_specs=[scalars()] + [whole()] * len(ins) + [pl.BlockSpec(memory_space=pl.ANY)] * len(after),
        out_specs=[whole()] * len(outs),
        **params(0, 2 * MIB),
    )(place, *ins, *after)


def named(number_ref, half):
    row = number_ref[pl.ds(half, 1), :].astype(jnp.float32)
    return jnp.broadcast_to(row, (16, HALF)).astype(HALF_TYPE)


def run(made, sems):
    made = [pltpu.make_async_copy(a, b, sems.at[i]) for i, (a, b) in enumerate(made)]
    for one in made:
        one.start()
    return made


def load(place, keys, values, query):
    def kernel(place_ref, k_ref, v_ref, q_ref, near, away, sems):
        c = place_ref[1]
        made = []
        for side, out in ((1 - c, away), (c, near)):
            for i, ref in enumerate((k_ref, v_ref, q_ref)):
                made.append((ref.at[half_rows(side)], out.at[pl.ds(i * HALF, HALF)]))
        for one in run(made, sems):
            one.wait()

    return pl.pallas_call(
        kernel,
        out_shape=[shaped(3 * HALF, 4 * HEAD_DIM)] * 2,
        in_specs=[scalars()] + [pl.BlockSpec(memory_space=pl.ANY)] * 3,
        out_specs=[whole()] * 2,
        scratch_shapes=[pltpu.SemaphoreType.DMA((6,))],
        **params(0, 6 * MIB, 56),
    )(place, keys, values, query)


def load_cross(cross_keys, cross_values, numbers, targets, after):
    def kernel(xk_ref, xv_ref, id_ref, t_ref, _, heads, sems):
        made = []
        for j in range(4):
            for ref, row in ((xk_ref, 0), (xv_ref, X_V)):
                made.append((ref.at[:, columns(j)], heads.at[j, pl.ds(row, 2 * HALF)]))
            for z in range(8):
                made.append((t_ref.at[z, :, columns(j)], heads.at[j, pl.ds(X_T + z * TGT, TGT)]))
        made = run(made, sems)
        for j in range(4):
            for half in (0, 1):
                heads[j, X_ID:X_T, half * HALF : half * HALF + HALF] = named(id_ref, half)
        for one in made:
            one.wait()

    anywhere = pl.BlockSpec(memory_space=pl.ANY)
    return pl.pallas_call(
        kernel,
        out_shape=shaped(4, X_ROWS, HEAD_DIM),
        in_specs=[anywhere, anywhere, whole(), anywhere, anywhere],
        out_specs=whole(),
        scratch_shapes=[pltpu.SemaphoreType.DMA((40,))],
        **params(0, 4 * MIB, 56),
    )(cross_keys, cross_values, numbers, targets, after)


class Either:
    def __init__(self, first, a, b):
        self.first, self.a, self.b = first, a, b

    def __getitem__(self, key):
        return jnp.where(self.first, self.a[key], self.b[key])


class Row:
    def __init__(self, ref, half):
        self.ref, self.half = ref, half

    def __getitem__(self, key):
        row = named(self.ref, self.half)
        return jnp.concatenate([row, row], axis=1)


def plan_pack(shifts, at, ins, outs):
    z, c, _ = at
    near, swapped, ids = ins
    pairs = []
    for k, d in enumerate(shifts):
        head = lax.rem(z + d, 8)
        column = rows_at(lax.rem(head, 4), HEAD_DIM, HEAD_DIM)
        first = (head // 4) == c
        for i, row in enumerate((0, ROW_V, ROW_Q)):
            part = (pl.ds(i * HALF, HALF), column)
            pairs.append((Either(first, near.at[part], swapped.at[part]), outs[k].at[pl.ds(row, HALF)]))
        pairs.append((Row(ids, c), outs[k].at[pl.ds(ROW_ID, 16)]))
    return pairs


def plan_first(at, ins, outs):
    group, ask = outs
    pairs = []
    for i, ref in enumerate(ins):
        pairs.append((ref.at[pl.ds(0, KEYS)], group.at[i]))
        pairs.append((ref.at[pl.ds(ROW_ID, ASK)], ask.at[i]))
    return pairs


def plan_second(at, ins, outs):
    chunks, (left, right, ask_first) = ins[:3], ins[3:]
    to_right, to_left, ask = outs
    pairs = [
        (left.at[pl.ds(0, 3)], to_right.at[pl.ds(0, 3)]),
        (right.at[pl.ds(3, 2)], to_left.at[pl.ds(0, 2)]),
        (ask_first, ask.at[pl.ds(0, 5)]),
    ]
    for i, ref in enumerate(chunks):
        pairs.append((ref.at[pl.ds(0, KEYS)], to_right.at[3 + i]))
        pairs.append((ref.at[pl.ds(0, KEYS)], to_left.at[2 + i]))
        pairs.append((ref.at[pl.ds(ROW_ID, ASK)], ask.at[5 + i]))
    return pairs


def plan_third(at, ins, outs):
    return [(ins[0].at[pl.ds(3, 1)], outs[0]), (ins[1].at[pl.ds(3, 2)], outs[1])]


def plan_targets(at, ins, outs):
    return [
        (ins[0].at[x, pl.ds(X_T + z * TGT, TGT)], outs[0].at[z, pl.ds(x * TGT, TGT)])
        for x in range(4)
        for z in range(8)
    ]


def plan_cross_back(at, ins, outs):
    x = at[2]
    return [
        (ins[0].at[rows_at(lax.rem(x + 4 - d, 4), TGT, TGT)], out) for d, out in zip(X_ORDER, outs, strict=True)
    ]


def plan_back_swap(at, ins, outs):
    return [(ins[0].at[pl.ds(4 * (1 - at[1]), 4)], outs[0])]


def plan_unpack(at, ins, outs):
    c = at[1]
    pairs = []
    back, swapped = ins[:2]
    for j in range(4):
        pairs.append((back.at[4 * c + j], outs[0].at[half_rows(c), columns(j)]))
        pairs.append((swapped.at[j], outs[0].at[half_rows(1 - c), columns(j)]))
    return pairs


def plan_cross_unpack(at, ins, outs):
    pairs = []
    for piece, shift in zip(ins, X_ORDER, strict=True):
        column = rows_at(lax.rem(at[2] + shift, 4), HEAD_DIM, HEAD_DIM)
        pairs.append((piece, outs[0].at[:, column]))
    return pairs


def id_row(ref, start, lanes):
    return ref[start : start + 16, lanes].astype(jnp.float32)[0:1, :]


def attend_kernel(cross, parts, asks, has_carry, final, partner, *refs):
    refs = list(refs)
    place_ref = refs.pop(0) if partner else None
    q_refs = [refs.pop(0) for _ in range(asks)]
    id_ref = refs.pop(0) if cross else None
    key_refs = [refs.pop(0) for _ in parts]
    carry_refs = [refs.pop(0) if has_carry else None for _ in range(asks)]
    other_ref = refs.pop(0) if partner else None
    out_refs = refs
    keys, values, key_ids = [], [], []
    for ref, (start, count) in zip(key_refs, parts, strict=True):
        if cross:
            for i in range(count):
                keys.append(ref[i, 0:X_V, :])
                values.append(ref[i, X_V:X_ID, :])
                key_ids += [id_row(ref.at[i], X_ID, slice(j, j + 128)) for j in (0, 128)]
            continue
        for i in range(start, start + count):
            keys.append(ref[i, 0:HALF, :])
            values.append(ref[i, ROW_V : ROW_V + HALF, :])
            key_ids.append(id_row(ref.at[i], ROW_ID, slice(0, 128)))
    keys = jnp.concatenate(keys, axis=0)
    values = jnp.concatenate(values, axis=0)
    q_row = 0 if cross else ROW_Q - ROW_ID
    def step(ask, block):
        q_ref, carry_ref, out_ref = q_refs[ask], carry_refs[ask], out_refs[ask]
        rows = rows_at(block, 256, 256)
        chunk = 2 * block
        query = q_ref[pl.ds(chunk, 2), q_row : q_row + HALF, :].reshape(256, HEAD_DIM)
        query = query * jnp.bfloat16(HEAD_DIM**-0.5)
        query_ids = []
        for i in (chunk, chunk + 1):
            row = id_ref.at[i][0:1, :] if cross else id_row(q_ref.at[i], 0, slice(0, 128))
            query_ids.append(jnp.transpose(jnp.broadcast_to(row, (128, 128))))
        query_ids = jnp.concatenate(query_ids, axis=0)
        match = jnp.concatenate([query_ids == ids for ids in key_ids], axis=1)
        scores = lax.dot_general(
            query, keys, (((1,), (1,)), ((), ())), preferred_element_type=jnp.float32
        )
        scores = jnp.where(match, scores, NEG)
        top = jnp.max(scores, axis=1, keepdims=True)
        if has_carry:
            old = carry_ref[rows, HEAD_DIM : HEAD_DIM + 1]
            top = jnp.maximum(top, old)
        else:
            top = jnp.maximum(top, LOW)
        weights = jnp.exp(scores - top)
        total = jnp.sum(weights, axis=1, keepdims=True)
        summed = jnp.dot(
            weights.astype(jnp.bfloat16), values, preferred_element_type=jnp.float32
        )
        if has_carry:
            scale = jnp.exp(old - top)
            total = total + scale * carry_ref[rows, HEAD_DIM + 64 : HEAD_DIM + 65]
            summed = summed + scale * carry_ref[rows, 0:HEAD_DIM]
        lane = lax.broadcasted_iota(jnp.int32, (256, 128), 1)
        if not final:
            out_ref[rows, 0:HEAD_DIM] = summed
            out_ref[rows, HEAD_DIM:WIDE] = jnp.where(lane < 64, top, total)
            return
        some = total > 0.0
        safe = jnp.where(some, total, 1.0)
        level = jnp.where(some, top + jnp.log(safe), NEG)
        summed = summed * (1.0 / safe)
        if partner:
            theirs_out = other_ref[pl.ds(chunk, 2)].reshape(256, WIDE)
            other = level_of(theirs_out[:, HEAD_DIM:WIDE])
            both = jnp.maximum(level, other)
            mine, theirs = jnp.exp(level - both), jnp.exp(other - both)
            share = 1.0 / (mine + theirs)
            summed = (mine * share) * summed + (theirs * share) * theirs_out[:, 0:HEAD_DIM].astype(jnp.float32)
            for half in (0, 1):
                to = lax.rem(place_ref[0] + 8 - ORDER[chunk + half], 8)
                out_ref[to] = summed[half * HALF : half * HALF + HALF].astype(jnp.bfloat16)
        else:
            high = level.astype(jnp.bfloat16).astype(jnp.float32)
            middle = (level - high).astype(jnp.bfloat16).astype(jnp.float32)
            low = level - high - middle
            three = jnp.where(lane < 32, high, jnp.where(lane < 64, middle, low))
            for half in (0, 1):
                pick = slice(half * HALF, half * HALF + HALF)
                out_ref[chunk + half, :, 0:HEAD_DIM] = summed[pick].astype(jnp.bfloat16)
                out_ref[chunk + half, :, HEAD_DIM:WIDE] = three[pick].astype(jnp.bfloat16)

    each = 2

    def body(i, _):
        for ask in range(asks):
            for sub in range(each):
                step(ask, each * i + sub)
        return 0

    if partner:
        for block in range(4):
            step(0, block)
    else:
        lax.fori_loop(0, 4 // each, body, 0)


def level_of(lanes):
    lanes = lanes.astype(jnp.float32)
    return (lanes[:, 0:1] + lanes[:, 32:33]) + lanes[:, 64:65]


def attend(queries, keys, ids=None, carry=(), final=False, other=None, place=None):
    arrays = [array for array, _, _ in keys]
    operands = [*queries] + ([] if ids is None else [ids]) + arrays + [*carry]
    operands += [] if other is None else [other]
    aliases = {}
    if carry and not final:
        aliases = {len(queries) + len(keys) + i: i for i in range(len(queries))}
    if not final:
        out = jax.ShapeDtypeStruct((1024, WIDE), jnp.float32)
    elif other is None:
        out = shaped(8, HALF, WIDE)
    else:
        out = shaped(8, HALF, HEAD_DIM)
    parts = tuple((start, count) for _, start, count in keys)
    width = sum(count for _, count in parts) * HALF * (1 if ids is None else 2)
    specs = [whole()] * len(operands)
    if other is not None:
        operands, specs = [place] + operands, [scalars()] + specs
    return pl.pallas_call(
        functools.partial(
            attend_kernel, ids is not None, parts, len(queries), len(carry) > 0, final, other is not None
        ),
        out_shape=[out] * len(queries),
        in_specs=specs,
        out_specs=[whole()] * len(queries),
        input_output_aliases=aliases,
        **params(4 * 1024 * len(queries) * width * HEAD_DIM, 4 * MIB, 24),
    )(*operands)


def finish_kernel(place_ref, carry_ref, other_ref, out_ref):
    for chunk in range(8):
        rows = slice(chunk * HALF, chunk * HALF + HALF)
        top = carry_ref[rows, HEAD_DIM : HEAD_DIM + 1]
        total = carry_ref[rows, HEAD_DIM + 64 : HEAD_DIM + 65]
        some = total > 0.0
        safe = jnp.where(some, total, 1.0)
        level = jnp.where(some, top + jnp.log(safe), NEG)
        other = level_of(other_ref[chunk, :, HEAD_DIM:WIDE])
        both = jnp.maximum(level, other)
        mine, theirs = jnp.exp(level - both), jnp.exp(other - both)
        share = 1.0 / (mine + theirs)
        summed = (mine * share / safe) * carry_ref[rows, 0:HEAD_DIM]
        summed += (theirs * share) * other_ref[chunk, :, 0:HEAD_DIM].astype(jnp.float32)
        out_ref[lax.rem(place_ref[0] + 8 - ORDER[chunk], 8)] = summed.astype(jnp.bfloat16)


def finish(place, carry, other):
    return pl.pallas_call(
        finish_kernel,
        out_shape=shaped(8, HALF, HEAD_DIM),
        in_specs=[scalars(), whole(), whole()],
        out_specs=whole(),
        **params(0, 3 * MIB),
    )(place, carry, other)


def merge_kernel(part_ref, out_ref):
    levels = [level_of(part_ref[i, :, HEAD_DIM:WIDE]) for i in range(8)]
    top = functools.reduce(jnp.maximum, levels)
    shares = [jnp.exp(level - top) for level in levels]
    summed = sum(
        share * part_ref[i, :, 0:HEAD_DIM].astype(jnp.float32) for i, share in enumerate(shares)
    )
    out_ref[...] = (summed * (1.0 / sum(shares))).astype(jnp.bfloat16)


def merge(part):
    return pl.pallas_call(
        merge_kernel,
        out_shape=shaped(HALF, HEAD_DIM),
        in_specs=[whole()],
        out_specs=whole(),
        **params(0, 2 * MIB),
    )(part)


def per_device(
    enc_query,
    enc_key,
    enc_value,
    input_segments,
    doc_bounds,
    target_query,
    cross_key,
    cross_value,
    target_segments,
):
    del doc_bounds
    ix, iz, ic = lax.axis_index("x"), lax.axis_index("z"), lax.axis_index("core")
    place = jnp.stack([iz, ic, ix]).astype(jnp.int32)
    local = functools.partial(copies, place)
    numbers = input_segments.reshape(2, HALF)
    target_ids = target_segments.reshape(4, 8, TGT).transpose(1, 0, 2).astype(jnp.float32)
    target_ids = jnp.broadcast_to(target_ids.reshape(8, 1, 128), (8, 8, 128))

    spread = jnp.broadcast_to(target_query[None], (8, TGT, 4 * HEAD_DIM))
    spread = lax.all_to_all(spread, "z", 0, 0, tiled=True)
    near, away = load(place, enc_key, enc_value, enc_query)
    swapped = core_swap(away)
    def packed(shifts, after=()):
        plan = functools.partial(plan_pack, shifts)
        return local(plan, [near, swapped, numbers], [(ROWS, HEAD_DIM)] * len(shifts), after)

    sent = packed(ORDER[:5])
    got = [sent[0]] + [z_send(sent[k], ORDER[k]) for k in range(1, 5)]
    heads = load_cross(cross_key, cross_value, numbers, spread, got[3])
    cross = lax.all_to_all(heads, "x", 0, 0, tiled=True)
    group, ask = local(plan_first, got, [(5, KEYS, HEAD_DIM), (5, ASK, HEAD_DIM)], [heads])


    sent = packed(ORDER[5:], [got[3]])
    rest = [z_send(chunk, d) for chunk, d in zip(sent, ORDER[5:], strict=True)]
    left, right = x_send(group, 1), x_send(group, 3)
    to_right, to_left, mine = local(
        plan_second,
        [*rest, left, right, ask],
        [(6, KEYS, HEAD_DIM), (5, KEYS, HEAD_DIM), (8, ASK, HEAD_DIM)],
    )

    from_left, from_right = x_send(to_right, 1), x_send(to_left, 3)
    theirs = core_swap(mine)
    (targets,) = local(plan_targets, [cross], [(8, HALF, HEAD_DIM)], [to_right])
    (part,) = attend([targets], [(cross, 0, 4)], ids=target_ids, final=True)
    part = lax.all_to_all(part, "z", 0, 0, tiled=True)
    queries = (mine, theirs)
    carry = attend(queries, [(group, 0, 5), (to_right, 3, 3), (left, 0, 5), (right, 0, 5)])
    lasts = local(
        plan_third, [from_left, from_right], [(1, KEYS, HEAD_DIM), (2, KEYS, HEAD_DIM)], [carry[0]]
    )

    far = [x_send(lasts[0], 1), x_send(lasts[1], 3)]
    carry = attend(queries, [(from_left, 0, 6), (from_right, 0, 5)], carry=carry)
    far_keys = [(far[0], 0, 1), (far[1], 0, 2)]
    (partial,) = attend([theirs], far_keys, carry=carry[1:], final=True)
    (last,) = attend([mine], far_keys, carry=carry[:1])
    back = finish(place, last, core_swap(partial))

    merged = merge(part)
    blocks = local(plan_cross_back, [merged], [(TGT, HEAD_DIM)] * 4, [back])
    blocks = [x_send(b, -d) if d else b for b, d in zip(blocks, X_ORDER, strict=True)]
    back = lax.all_to_all(back, "z", 0, 0, tiled=True)
    (away,) = local(plan_back_swap, [back], [(4, HALF, HEAD_DIM)], blocks)
    (enc_out,) = local(plan_unpack, [back, core_swap(away)], [(2 * HALF, 4 * HEAD_DIM)])
    (cross_out,) = local(plan_cross_unpack, blocks, [(TGT, 4 * HEAD_DIM)])
    return enc_out, cross_out


def solution(mesh):
    shape = mesh.shape
    split = Mesh(
        mesh.devices.reshape(4, shape["ctx"] // 4, shape["head"], shape["dp"]), ("x", "z", "core", "dp")
    )
    tokens = P(("dp", "x", "z"), "core")
    placed = (
        tokens,
        tokens,
        tokens,
        P(("dp", "x", "z")),
        P(("dp", "x", "z"), None),
        tokens,
        tokens,
        tokens,
        P("dp"),
    )
    return jax.shard_map(
        per_device, mesh=split, in_specs=placed, out_specs=(tokens, tokens), check_vma=False
    )
```

```python
import functools

import jax
import jax.numpy as jnp
from jax import lax
from jax.experimental import pallas as pl
from jax.experimental.pallas import tpu as pltpu
from jax.sharding import Mesh
from jax.sharding import PartitionSpec as P

HEAD_DIM = 256
HALF = 128
TGT = 32
NEG = -1.0e30
LOW = -1.0e29

ROW_V = HALF
ROW_ID = 2 * HALF
ROW_Q = ROW_ID + 16
ROWS = ROW_Q + HALF
KEYS = ROW_Q
ASK = ROWS - ROW_ID
X_V = 2 * HALF
X_ID = 4 * HALF
X_T = X_ID + 16
X_ROWS = X_T + 8 * TGT
ORDER = (0, 2, 6, 1, 7, 3, 5, 4)
X_ORDER = (0, 1, 3, 2)
WIDE = HEAD_DIM + 128
MIB = 1024 * 1024
HALF_TYPE = jnp.bfloat16


def z_send(array, shift):
    return lax.ppermute(array, "z", [(i, (i + shift) % 8) for i in range(8)])


def x_send(array, shift):
    return lax.ppermute(array, "x", [(i, (i + shift) % 4) for i in range(4)])


def core_swap(array):
    return lax.ppermute(array, "core", [(0, 1), (1, 0)])


def params(flops, moved, limit=8):
    return dict(
        compiler_params=pltpu.CompilerParams(vmem_limit_bytes=limit * MIB),
        cost_estimate=pl.CostEstimate(flops=flops, bytes_accessed=moved, transcendentals=0),
    )


def rows_at(start, size, unit):
    if isinstance(start, int):
        return pl.ds(start * unit, size)
    return pl.ds(pl.multiple_of(start * unit, unit), size)


def half_rows(c):
    return rows_at(c, HALF, HALF)


def columns(j):
    return pl.ds(j * HEAD_DIM, HEAD_DIM)


def whole():
    return pl.BlockSpec(memory_space=pltpu.VMEM)


def scalars():
    return pl.BlockSpec(memory_space=pltpu.SMEM)


def shaped(*shape):
    return jax.ShapeDtypeStruct(shape, HALF_TYPE)


def copy(a, b):
    b[...] = a[...]


def copies(place, plan, ins, outs, after=()):
    def kernel(place_ref, *refs):
        at = (place_ref[0], place_ref[1], place_ref[2])
        for a, b, *when in plan(at, refs[: len(ins)], refs[len(ins) + len(after) :]):
            if when:
                pl.when(when[0])(functools.partial(copy, a, b))
            else:
                copy(a, b)

    return pl.pallas_call(
        kernel,
        out_shape=[shaped(*shape) for shape in outs],
        in_specs=[scalars()] + [whole()] * len(ins) + [pl.BlockSpec(memory_space=pl.ANY)] * len(after),
        out_specs=[whole()] * len(outs),
        **params(0, 2 * MIB),
    )(place, *ins, *after)


def named(number_ref, half):
    row = number_ref[pl.ds(half, 1), :].astype(jnp.float32)
    return jnp.broadcast_to(row, (16, HALF)).astype(HALF_TYPE)


def run(made, sems):
    made = [pltpu.make_async_copy(a, b, sems.at[i]) for i, (a, b) in enumerate(made)]
    for one in made:
        one.start()
    return made


def load(place, keys, values, query):
    def kernel(place_ref, k_ref, v_ref, q_ref, near, away, sems):
        c = place_ref[1]
        made = []
        for side, out in ((1 - c, away), (c, near)):
            for i, ref in enumerate((k_ref, v_ref, q_ref)):
                made.append((ref.at[half_rows(side)], out.at[pl.ds(i * HALF, HALF)]))
        for one in run(made, sems):
            one.wait()

    return pl.pallas_call(
        kernel,
        out_shape=[shaped(3 * HALF, 4 * HEAD_DIM)] * 2,
        in_specs=[scalars()] + [pl.BlockSpec(memory_space=pl.ANY)] * 3,
        out_specs=[whole()] * 2,
        scratch_shapes=[pltpu.SemaphoreType.DMA((6,))],
        **params(0, 6 * MIB, 56),
    )(place, keys, values, query)


def load_cross(cross_keys, cross_values, numbers, targets, after):
    def kernel(xk_ref, xv_ref, id_ref, t_ref, _, heads, sems):
        made = []
        for j in range(4):
            for ref, row in ((xk_ref, 0), (xv_ref, X_V)):
                made.append((ref.at[:, columns(j)], heads.at[j, pl.ds(row, 2 * HALF)]))
            for z in range(8):
                made.append((t_ref.at[z, :, columns(j)], heads.at[j, pl.ds(X_T + z * TGT, TGT)]))
        made = run(made, sems)
        for j in range(4):
            for half in (0, 1):
                heads[j, X_ID:X_T, half * HALF : half * HALF + HALF] = named(id_ref, half)
        for one in made:
            one.wait()

    anywhere = pl.BlockSpec(memory_space=pl.ANY)
    return pl.pallas_call(
        kernel,
        out_shape=shaped(4, X_ROWS, HEAD_DIM),
        in_specs=[anywhere, anywhere, whole(), anywhere, anywhere],
        out_specs=whole(),
        scratch_shapes=[pltpu.SemaphoreType.DMA((40,))],
        **params(0, 4 * MIB, 56),
    )(cross_keys, cross_values, numbers, targets, after)


class Either:
    def __init__(self, first, a, b):
        self.first, self.a, self.b = first, a, b

    def __getitem__(self, key):
        return jnp.where(self.first, self.a[key], self.b[key])


class Row:
    def __init__(self, ref, half):
        self.ref, self.half = ref, half

    def __getitem__(self, key):
        row = named(self.ref, self.half)
        return jnp.concatenate([row, row], axis=1)


def plan_pack(shifts, at, ins, outs):
    z, c, _ = at
    near, swapped, ids = ins
    pairs = []
    for k, d in enumerate(shifts):
        head = lax.rem(z + d, 8)
        column = rows_at(lax.rem(head, 4), HEAD_DIM, HEAD_DIM)
        first = (head // 4) == c
        for i, row in enumerate((0, ROW_V, ROW_Q)):
            part = (pl.ds(i * HALF, HALF), column)
            pairs.append((Either(first, near.at[part], swapped.at[part]), outs[k].at[pl.ds(row, HALF)]))
        pairs.append((Row(ids, c), outs[k].at[pl.ds(ROW_ID, 16)]))
    return pairs


def plan_first(at, ins, outs):
    group, ask = outs
    pairs = []
    for i, ref in enumerate(ins):
        pairs.append((ref.at[pl.ds(0, KEYS)], group.at[i]))
        pairs.append((ref.at[pl.ds(ROW_ID, ASK)], ask.at[i]))
    return pairs


def plan_second(at, ins, outs):
    chunks, (left, right, ask_first) = ins[:3], ins[3:]
    to_right, to_left, ask = outs
    pairs = [
        (left.at[pl.ds(0, 3)], to_right.at[pl.ds(0, 3)]),
        (right.at[pl.ds(3, 2)], to_left.at[pl.ds(0, 2)]),
        (ask_first, ask.at[pl.ds(0, 5)]),
    ]
    for i, ref in enumerate(chunks):
        pairs.append((ref.at[pl.ds(0, KEYS)], to_right.at[3 + i]))
        pairs.append((ref.at[pl.ds(0, KEYS)], to_left.at[2 + i]))
        pairs.append((ref.at[pl.ds(ROW_ID, ASK)], ask.at[5 + i]))
    return pairs


def plan_third(at, ins, outs):
    return [(ins[0].at[pl.ds(3, 1)], outs[0]), (ins[1].at[pl.ds(3, 2)], outs[1])]


def plan_targets(at, ins, outs):
    return [
        (ins[0].at[x, pl.ds(X_T + z * TGT, TGT)], outs[0].at[z, pl.ds(x * TGT, TGT)])
        for x in range(4)
        for z in range(8)
    ]


def plan_cross_back(at, ins, outs):
    x = at[2]
    return [
        (ins[0].at[rows_at(lax.rem(x + 4 - d, 4), TGT, TGT)], out) for d, out in zip(X_ORDER, outs, strict=True)
    ]


def plan_back_swap(at, ins, outs):
    return [(ins[0].at[pl.ds(4 * (1 - at[1]), 4)], outs[0])]


def plan_unpack(at, ins, outs):
    c = at[1]
    pairs = []
    back, swapped = ins[:2]
    for j in range(4):
        pairs.append((back.at[4 * c + j], outs[0].at[half_rows(c), columns(j)]))
        pairs.append((swapped.at[j], outs[0].at[half_rows(1 - c), columns(j)]))
    return pairs


def plan_cross_unpack(at, ins, outs):
    pairs = []
    for piece, shift in zip(ins, X_ORDER, strict=True):
        column = rows_at(lax.rem(at[2] + shift, 4), HEAD_DIM, HEAD_DIM)
        pairs.append((piece, outs[0].at[:, column]))
    return pairs


def id_row(ref, start, lanes):
    return ref[start : start + 16, lanes].astype(jnp.float32)[0:1, :]


def attend_kernel(cross, parts, asks, has_carry, final, partner, *refs):
    refs = list(refs)
    place_ref = refs.pop(0) if partner else None
    q_refs = [refs.pop(0) for _ in range(asks)]
    id_ref = refs.pop(0) if cross else None
    key_refs = [refs.pop(0) for _ in parts]
    carry_refs = [refs.pop(0) if has_carry else None for _ in range(asks)]
    other_ref = refs.pop(0) if partner else None
    out_refs = refs
    keys, values, key_ids = [], [], []
    for ref, (start, count) in zip(key_refs, parts, strict=True):
        if cross:
            for i in range(count):
                keys.append(ref[i, 0:X_V, :])
                values.append(ref[i, X_V:X_ID, :])
                key_ids += [id_row(ref.at[i], X_ID, slice(j, j + 128)) for j in (0, 128)]
            continue
        for i in range(start, start + count):
            keys.append(ref[i, 0:HALF, :])
            values.append(ref[i, ROW_V : ROW_V + HALF, :])
            key_ids.append(id_row(ref.at[i], ROW_ID, slice(0, 128)))
    keys = jnp.concatenate(keys, axis=0)
    values = jnp.concatenate(values, axis=0)
    q_row = 0 if cross else ROW_Q - ROW_ID
    def step(ask, block):
        q_ref, carry_ref, out_ref = q_refs[ask], carry_refs[ask], out_refs[ask]
        rows = rows_at(block, 256, 256)
        chunk = 2 * block
        query = q_ref[pl.ds(chunk, 2), q_row : q_row + HALF, :].reshape(256, HEAD_DIM)
        query = query * jnp.bfloat16(HEAD_DIM**-0.5)
        query_ids = []
        for i in (chunk, chunk + 1):
            row = id_ref.at[i][0:1, :] if cross else id_row(q_ref.at[i], 0, slice(0, 128))
            query_ids.append(jnp.transpose(jnp.broadcast_to(row, (128, 128))))
        query_ids = jnp.concatenate(query_ids, axis=0)
        match = jnp.concatenate([query_ids == ids for ids in key_ids], axis=1)
        scores = lax.dot_general(
            query, keys, (((1,), (1,)), ((), ())), preferred_element_type=jnp.float32
        )
        scores = jnp.where(match, scores, NEG)
        top = jnp.max(scores, axis=1, keepdims=True)
        if has_carry:
            old = carry_ref[rows, HEAD_DIM : HEAD_DIM + 1]
            top = jnp.maximum(top, old)
        else:
            top = jnp.maximum(top, LOW)
        weights = jnp.exp(scores - top)
        total = jnp.sum(weights, axis=1, keepdims=True)
        summed = jnp.dot(
            weights.astype(jnp.bfloat16), values, preferred_element_type=jnp.float32
        )
        if has_carry:
            scale = jnp.exp(old - top)
            total = total + scale * carry_ref[rows, HEAD_DIM + 64 : HEAD_DIM + 65]
            summed = summed + scale * carry_ref[rows, 0:HEAD_DIM]
        lane = lax.broadcasted_iota(jnp.int32, (256, 128), 1)
        if not final:
            out_ref[rows, 0:HEAD_DIM] = summed
            out_ref[rows, HEAD_DIM:WIDE] = jnp.where(lane < 64, top, total)
            return
        some = total > 0.0
        safe = jnp.where(some, total, 1.0)
        level = jnp.where(some, top + jnp.log(safe), NEG)
        summed = summed * (1.0 / safe)
        if partner:
            theirs_out = other_ref[pl.ds(chunk, 2)].reshape(256, WIDE)
            other = level_of(theirs_out[:, HEAD_DIM:WIDE])
            both = jnp.maximum(level, other)
            mine, theirs = jnp.exp(level - both), jnp.exp(other - both)
            share = 1.0 / (mine + theirs)
            summed = (mine * share) * summed + (theirs * share) * theirs_out[:, 0:HEAD_DIM].astype(jnp.float32)
            for half in (0, 1):
                to = lax.rem(place_ref[0] + 8 - ORDER[chunk + half], 8)
                out_ref[to] = summed[half * HALF : half * HALF + HALF].astype(jnp.bfloat16)
        else:
            high = level.astype(jnp.bfloat16).astype(jnp.float32)
            middle = (level - high).astype(jnp.bfloat16).astype(jnp.float32)
            low = level - high - middle
            three = jnp.where(lane < 32, high, jnp.where(lane < 64, middle, low))
            for half in (0, 1):
                pick = slice(half * HALF, half * HALF + HALF)
                out_ref[chunk + half, :, 0:HEAD_DIM] = summed[pick].astype(jnp.bfloat16)
                out_ref[chunk + half, :, HEAD_DIM:WIDE] = three[pick].astype(jnp.bfloat16)

    each = 2

    def body(i, _):
        for ask in range(asks):
            for sub in range(each):
                step(ask, each * i + sub)
        return 0

    if partner:
        for block in range(4):
            step(0, block)
    else:
        lax.fori_loop(0, 4 // each, body, 0)


def level_of(lanes):
    lanes = lanes.astype(jnp.float32)
    return (lanes[:, 0:1] + lanes[:, 32:33]) + lanes[:, 64:65]


def attend(queries, keys, ids=None, carry=(), final=False, other=None, place=None):
    arrays = [array for array, _, _ in keys]
    operands = [*queries] + ([] if ids is None else [ids]) + arrays + [*carry]
    operands += [] if other is None else [other]
    aliases = {}
    if carry and not final:
        aliases = {len(queries) + len(keys) + i: i for i in range(len(queries))}
    if not final:
        out = jax.ShapeDtypeStruct((1024, WIDE), jnp.float32)
    elif other is None:
        out = shaped(8, HALF, WIDE)
    else:
        out = shaped(8, HALF, HEAD_DIM)
    parts = tuple((start, count) for _, start, count in keys)
    width = sum(count for _, count in parts) * HALF * (1 if ids is None else 2)
    specs = [whole()] * len(operands)
    if other is not None:
        operands, specs = [place] + operands, [scalars()] + specs
    return pl.pallas_call(
        functools.partial(
            attend_kernel, ids is not None, parts, len(queries), len(carry) > 0, final, other is not None
        ),
        out_shape=[out] * len(queries),
        in_specs=specs,
        out_specs=[whole()] * len(queries),
        input_output_aliases=aliases,
        **params(4 * 1024 * len(queries) * width * HEAD_DIM, 4 * MIB, 24),
    )(*operands)


def merge_kernel(part_ref, out_ref):
    levels = [level_of(part_ref[i, :, HEAD_DIM:WIDE]) for i in range(8)]
    top = functools.reduce(jnp.maximum, levels)
    shares = [jnp.exp(level - top) for level in levels]
    summed = sum(
        share * part_ref[i, :, 0:HEAD_DIM].astype(jnp.float32) for i, share in enumerate(shares)
    )
    out_ref[...] = (summed * (1.0 / sum(shares))).astype(jnp.bfloat16)


def merge(part):
    return pl.pallas_call(
        merge_kernel,
        out_shape=shaped(HALF, HEAD_DIM),
        in_specs=[whole()],
        out_specs=whole(),
        **params(0, 2 * MIB),
    )(part)


def per_device(
    enc_query,
    enc_key,
    enc_value,
    input_segments,
    doc_bounds,
    target_query,
    cross_key,
    cross_value,
    target_segments,
):
    del doc_bounds
    ix, iz, ic = lax.axis_index("x"), lax.axis_index("z"), lax.axis_index("core")
    place = jnp.stack([iz, ic, ix]).astype(jnp.int32)
    local = functools.partial(copies, place)
    numbers = input_segments.reshape(2, HALF)
    target_ids = target_segments.reshape(4, 8, TGT).transpose(1, 0, 2).astype(jnp.float32)
    target_ids = jnp.broadcast_to(target_ids.reshape(8, 1, 128), (8, 8, 128))

    spread = jnp.broadcast_to(target_query[None], (8, TGT, 4 * HEAD_DIM))
    spread = lax.all_to_all(spread, "z", 0, 0, tiled=True)
    near, away = load(place, enc_key, enc_value, enc_query)
    swapped = core_swap(away)
    def packed(shifts, after=()):
        plan = functools.partial(plan_pack, shifts)
        return local(plan, [near, swapped, numbers], [(ROWS, HEAD_DIM)] * len(shifts), after)

    sent = packed(ORDER[:5])
    got = [sent[0]] + [z_send(sent[k], ORDER[k]) for k in range(1, 5)]
    heads = load_cross(cross_key, cross_value, numbers, spread, got[3])
    cross = lax.all_to_all(heads, "x", 0, 0, tiled=True)
    group, ask = local(plan_first, got, [(5, KEYS, HEAD_DIM), (5, ASK, HEAD_DIM)], [heads])


    sent = packed(ORDER[5:], [got[3]])
    rest = [z_send(chunk, d) for chunk, d in zip(sent, ORDER[5:], strict=True)]
    left, right = x_send(group, 1), x_send(group, 3)
    to_right, to_left, mine = local(
        plan_second,
        [*rest, left, right, ask],
        [(6, KEYS, HEAD_DIM), (5, KEYS, HEAD_DIM), (8, ASK, HEAD_DIM)],
    )

    from_left, from_right = x_send(to_right, 1), x_send(to_left, 3)
    theirs = core_swap(mine)
    (targets,) = local(plan_targets, [cross], [(8, HALF, HEAD_DIM)], [to_right])
    (part,) = attend([targets], [(cross, 0, 4)], ids=target_ids, final=True)
    part = lax.all_to_all(part, "z", 0, 0, tiled=True)
    queries = (mine, theirs)
    carry = attend(queries, [(group, 0, 5), (to_right, 3, 3), (left, 0, 5), (right, 0, 5)])
    lasts = local(
        plan_third, [from_left, from_right], [(1, KEYS, HEAD_DIM), (2, KEYS, HEAD_DIM)], [carry[0]]
    )

    far = [x_send(lasts[0], 1), x_send(lasts[1], 3)]
    carry = attend(queries, [(from_left, 0, 6), (from_right, 0, 5)], carry=carry)
    far_keys = [(far[0], 0, 1), (far[1], 0, 2)]
    (partial,) = attend([theirs], far_keys, carry=carry[1:], final=True)
    (back,) = attend([mine], far_keys, carry=carry[:1], final=True, other=core_swap(partial), place=place)

    merged = merge(part)
    blocks = local(plan_cross_back, [merged], [(TGT, HEAD_DIM)] * 4, [back])
    blocks = [x_send(b, -d) if d else b for b, d in zip(blocks, X_ORDER, strict=True)]
    back = lax.all_to_all(back, "z", 0, 0, tiled=True)
    (away,) = local(plan_back_swap, [back], [(4, HALF, HEAD_DIM)], blocks)
    (enc_out,) = local(plan_unpack, [back, core_swap(away)], [(2 * HALF, 4 * HEAD_DIM)])
    (cross_out,) = local(plan_cross_unpack, blocks, [(TGT, 4 * HEAD_DIM)])
    return enc_out, cross_out


def solution(mesh):
    shape = mesh.shape
    split = Mesh(
        mesh.devices.reshape(4, shape["ctx"] // 4, shape["head"], shape["dp"]), ("x", "z", "core", "dp")
    )
    tokens = P(("dp", "x", "z"), "core")
    placed = (
        tokens,
        tokens,
        tokens,
        P(("dp", "x", "z")),
        P(("dp", "x", "z"), None),
        tokens,
        tokens,
        tokens,
        P("dp"),
    )
    return jax.shard_map(
        per_device, mesh=split, in_specs=placed, out_specs=(tokens, tokens), check_vma=False
    )
```

```python
import functools

import jax
import jax.numpy as jnp
from jax import lax
from jax.experimental import pallas as pl
from jax.experimental.pallas import tpu as pltpu
from jax.sharding import Mesh
from jax.sharding import PartitionSpec as P

HEAD_DIM = 256
HALF = 128
TGT = 32
NEG = -1.0e30
LOW = -1.0e29

ROW_V = HALF
ROW_ID = 2 * HALF
ROW_Q = ROW_ID + 16
ROWS = ROW_Q + HALF
KEYS = ROW_Q
ASK = ROWS - ROW_ID
X_V = 2 * HALF
X_ID = 4 * HALF
X_T = X_ID + 16
X_ROWS = X_T + 8 * TGT
ORDER = (0, 2, 6, 1, 7, 3, 5, 4)
X_ORDER = (0, 1, 3, 2)
WIDE = HEAD_DIM + 128
MIB = 1024 * 1024
HALF_TYPE = jnp.bfloat16


def z_send(array, shift):
    return lax.ppermute(array, "z", [(i, (i + shift) % 8) for i in range(8)])


def x_send(array, shift):
    return lax.ppermute(array, "x", [(i, (i + shift) % 4) for i in range(4)])


def core_swap(array):
    return lax.ppermute(array, "core", [(0, 1), (1, 0)])


def params(flops, moved, limit=8):
    return dict(
        compiler_params=pltpu.CompilerParams(vmem_limit_bytes=limit * MIB),
        cost_estimate=pl.CostEstimate(flops=flops, bytes_accessed=moved, transcendentals=0),
    )


def rows_at(start, size, unit):
    if isinstance(start, int):
        return pl.ds(start * unit, size)
    return pl.ds(pl.multiple_of(start * unit, unit), size)


def half_rows(c):
    return rows_at(c, HALF, HALF)


def columns(j):
    return pl.ds(j * HEAD_DIM, HEAD_DIM)


def whole():
    return pl.BlockSpec(memory_space=pltpu.VMEM)


def scalars():
    return pl.BlockSpec(memory_space=pltpu.SMEM)


def shaped(*shape):
    return jax.ShapeDtypeStruct(shape, HALF_TYPE)


def copy(a, b):
    b[...] = a[...]


def copies(place, plan, ins, outs, after=()):
    def kernel(place_ref, *refs):
        at = (place_ref[0], place_ref[1], place_ref[2])
        for a, b, *when in plan(at, refs[: len(ins)], refs[len(ins) + len(after) :]):
            if when:
                pl.when(when[0])(functools.partial(copy, a, b))
            else:
                copy(a, b)

    return pl.pallas_call(
        kernel,
        out_shape=[shaped(*shape) for shape in outs],
        in_specs=[scalars()] + [whole()] * len(ins) + [pl.BlockSpec(memory_space=pl.ANY)] * len(after),
        out_specs=[whole()] * len(outs),
        **params(0, 2 * MIB),
    )(place, *ins, *after)


def named(number_ref, half):
    row = number_ref[pl.ds(half, 1), :].astype(jnp.float32)
    return jnp.broadcast_to(row, (16, HALF)).astype(HALF_TYPE)


def run(made, sems):
    made = [pltpu.make_async_copy(a, b, sems.at[i]) for i, (a, b) in enumerate(made)]
    for one in made:
        one.start()
    return made


def load(place, keys, values, query):
    def kernel(place_ref, k_ref, v_ref, q_ref, near, away, sems):
        c = place_ref[1]
        made = []
        for side, out in ((1 - c, away), (c, near)):
            for i, ref in enumerate((k_ref, v_ref, q_ref)):
                made.append((ref.at[half_rows(side)], out.at[pl.ds(i * HALF, HALF)]))
        for one in run(made, sems):
            one.wait()

    return pl.pallas_call(
        kernel,
        out_shape=[shaped(3 * HALF, 4 * HEAD_DIM)] * 2,
        in_specs=[scalars()] + [pl.BlockSpec(memory_space=pl.ANY)] * 3,
        out_specs=[whole()] * 2,
        scratch_shapes=[pltpu.SemaphoreType.DMA((6,))],
        **params(0, 6 * MIB, 56),
    )(place, keys, values, query)


def load_cross(cross_keys, cross_values, numbers, after):
    def kernel(xk_ref, xv_ref, id_ref, _, heads, sems):
        made = []
        for j in range(4):
            for ref, row in ((xk_ref, 0), (xv_ref, X_V)):
                made.append((ref.at[:, columns(j)], heads.at[j, pl.ds(row, 2 * HALF)]))
        made = run(made, sems)
        for j in range(4):
            for half in (0, 1):
                heads[j, X_ID:X_T, half * HALF : half * HALF + HALF] = named(id_ref, half)
        heads[:, X_T:X_ROWS, :] = jnp.zeros((4, X_ROWS - X_T, HEAD_DIM), HALF_TYPE)
        for one in made:
            one.wait()

    anywhere = pl.BlockSpec(memory_space=pl.ANY)
    return pl.pallas_call(
        kernel,
        out_shape=shaped(4, X_ROWS, HEAD_DIM),
        in_specs=[anywhere, anywhere, whole(), anywhere],
        out_specs=whole(),
        scratch_shapes=[pltpu.SemaphoreType.DMA((8,))],
        **params(0, 4 * MIB, 56),
    )(cross_keys, cross_values, numbers, after)


def add_targets(heads, targets, after):
    def kernel(_, t_ref, __, out):
        for j in range(4):
            for z in range(8):
                out[j, X_T + z * TGT : X_T + (z + 1) * TGT, :] = t_ref[z, :, columns(j)]

    return pl.pallas_call(
        kernel,
        out_shape=shaped(4, X_ROWS, HEAD_DIM),
        in_specs=[whole(), whole(), pl.BlockSpec(memory_space=pl.ANY)],
        out_specs=whole(),
        input_output_aliases={0: 0},
        **params(0, 1 * MIB),
    )(heads, targets, after)


class Either:
    def __init__(self, first, a, b):
        self.first, self.a, self.b = first, a, b

    def __getitem__(self, key):
        return jnp.where(self.first, self.a[key], self.b[key])


class Row:
    def __init__(self, ref, half):
        self.ref, self.half = ref, half

    def __getitem__(self, key):
        row = named(self.ref, self.half)
        return jnp.concatenate([row, row], axis=1)


def plan_pack(shifts, at, ins, outs):
    z, c, _ = at
    near, swapped, ids = ins
    pairs = []
    for k, d in enumerate(shifts):
        head = lax.rem(z + d, 8)
        column = rows_at(lax.rem(head, 4), HEAD_DIM, HEAD_DIM)
        first = (head // 4) == c
        for i, row in enumerate((0, ROW_V, ROW_Q)):
            part = (pl.ds(i * HALF, HALF), column)
            pairs.append((Either(first, near.at[part], swapped.at[part]), outs[k].at[pl.ds(row, HALF)]))
        pairs.append((Row(ids, c), outs[k].at[pl.ds(ROW_ID, 16)]))
    return pairs


def plan_first(at, ins, outs):
    group, ask = outs
    pairs = []
    for i, ref in enumerate(ins):
        pairs.append((ref.at[pl.ds(0, KEYS)], group.at[i]))
        pairs.append((ref.at[pl.ds(ROW_ID, ASK)], ask.at[i]))
    return pairs


def plan_second(at, ins, outs):
    chunks, (left, right, ask_first) = ins[:3], ins[3:]
    to_right, to_left, ask = outs
    pairs = [
        (left.at[pl.ds(0, 3)], to_right.at[pl.ds(0, 3)]),
        (right.at[pl.ds(3, 2)], to_left.at[pl.ds(0, 2)]),
        (ask_first, ask.at[pl.ds(0, 5)]),
    ]
    for i, ref in enumerate(chunks):
        pairs.append((ref.at[pl.ds(0, KEYS)], to_right.at[3 + i]))
        pairs.append((ref.at[pl.ds(0, KEYS)], to_left.at[2 + i]))
        pairs.append((ref.at[pl.ds(ROW_ID, ASK)], ask.at[5 + i]))
    return pairs


def plan_third(at, ins, outs):
    return [(ins[0].at[pl.ds(3, 1)], outs[0]), (ins[1].at[pl.ds(3, 2)], outs[1])]


def plan_targets(at, ins, outs):
    return [
        (ins[0].at[x, pl.ds(X_T + z * TGT, TGT)], outs[0].at[z, pl.ds(x * TGT, TGT)])
        for x in range(4)
        for z in range(8)
    ]


def plan_cross_back(at, ins, outs):
    x = at[2]
    return [
        (ins[0].at[rows_at(lax.rem(x + 4 - d, 4), TGT, TGT)], out) for d, out in zip(X_ORDER, outs, strict=True)
    ]


def plan_back_swap(at, ins, outs):
    return [(ins[0].at[pl.ds(4 * (1 - at[1]), 4)], outs[0])]


def plan_unpack(at, ins, outs):
    c = at[1]
    pairs = []
    back, swapped = ins[:2]
    for j in range(4):
        pairs.append((back.at[4 * c + j], outs[0].at[half_rows(c), columns(j)]))
        pairs.append((swapped.at[j], outs[0].at[half_rows(1 - c), columns(j)]))
    return pairs


def plan_cross_unpack(at, ins, outs):
    pairs = []
    for piece, shift in zip(ins, X_ORDER, strict=True):
        column = rows_at(lax.rem(at[2] + shift, 4), HEAD_DIM, HEAD_DIM)
        pairs.append((piece, outs[0].at[:, column]))
    return pairs


def id_row(ref, start, lanes):
    return ref[start : start + 16, lanes].astype(jnp.float32)[0:1, :]


def attend_kernel(cross, parts, asks, has_carry, final, partner, *refs):
    refs = list(refs)
    place_ref = refs.pop(0) if partner else None
    q_refs = [refs.pop(0) for _ in range(asks)]
    id_ref = refs.pop(0) if cross else None
    key_refs = [refs.pop(0) for _ in parts]
    carry_refs = [refs.pop(0) if has_carry else None for _ in range(asks)]
    other_ref = refs.pop(0) if partner else None
    out_refs = refs
    keys, values, key_ids = [], [], []
    for ref, (start, count) in zip(key_refs, parts, strict=True):
        if cross:
            for i in range(count):
                keys.append(ref[i, 0:X_V, :])
                values.append(ref[i, X_V:X_ID, :])
                key_ids += [id_row(ref.at[i], X_ID, slice(j, j + 128)) for j in (0, 128)]
            continue
        for i in range(start, start + count):
            keys.append(ref[i, 0:HALF, :])
            values.append(ref[i, ROW_V : ROW_V + HALF, :])
            key_ids.append(id_row(ref.at[i], ROW_ID, slice(0, 128)))
    keys = jnp.concatenate(keys, axis=0)
    values = jnp.concatenate(values, axis=0)
    q_row = 0 if cross else ROW_Q - ROW_ID
    def step(ask, block):
        q_ref, carry_ref, out_ref = q_refs[ask], carry_refs[ask], out_refs[ask]
        rows = rows_at(block, 256, 256)
        chunk = 2 * block
        query = q_ref[pl.ds(chunk, 2), q_row : q_row + HALF, :].reshape(256, HEAD_DIM)
        query = query * jnp.bfloat16(HEAD_DIM**-0.5)
        query_ids = []
        for i in (chunk, chunk + 1):
            row = id_ref.at[i][0:1, :] if cross else id_row(q_ref.at[i], 0, slice(0, 128))
            query_ids.append(jnp.transpose(jnp.broadcast_to(row, (128, 128))))
        query_ids = jnp.concatenate(query_ids, axis=0)
        match = jnp.concatenate([query_ids == ids for ids in key_ids], axis=1)
        scores = lax.dot_general(
            query, keys, (((1,), (1,)), ((), ())), preferred_element_type=jnp.float32
        )
        scores = jnp.where(match, scores, NEG)
        top = jnp.max(scores, axis=1, keepdims=True)
        if has_carry:
            old = carry_ref[rows, HEAD_DIM : HEAD_DIM + 1]
            top = jnp.maximum(top, old)
        else:
            top = jnp.maximum(top, LOW)
        weights = jnp.exp(scores - top)
        total = jnp.sum(weights, axis=1, keepdims=True)
        summed = jnp.dot(
            weights.astype(jnp.bfloat16), values, preferred_element_type=jnp.float32
        )
        if has_carry:
            scale = jnp.exp(old - top)
            total = total + scale * carry_ref[rows, HEAD_DIM + 64 : HEAD_DIM + 65]
            summed = summed + scale * carry_ref[rows, 0:HEAD_DIM]
        lane = lax.broadcasted_iota(jnp.int32, (256, 128), 1)
        if not final:
            out_ref[rows, 0:HEAD_DIM] = summed
            out_ref[rows, HEAD_DIM:WIDE] = jnp.where(lane < 64, top, total)
            return
        some = total > 0.0
        safe = jnp.where(some, total, 1.0)
        level = jnp.where(some, top + jnp.log(safe), NEG)
        summed = summed * (1.0 / safe)
        if partner:
            theirs_out = other_ref[pl.ds(chunk, 2)].reshape(256, WIDE)
            other = level_of(theirs_out[:, HEAD_DIM:WIDE])
            both = jnp.maximum(level, other)
            mine, theirs = jnp.exp(level - both), jnp.exp(other - both)
            share = 1.0 / (mine + theirs)
            summed = (mine * share) * summed + (theirs * share) * theirs_out[:, 0:HEAD_DIM].astype(jnp.float32)
            for half in (0, 1):
                to = lax.rem(place_ref[0] + 8 - ORDER[chunk + half], 8)
                out_ref[to] = summed[half * HALF : half * HALF + HALF].astype(jnp.bfloat16)
        else:
            high = level.astype(jnp.bfloat16).astype(jnp.float32)
            middle = (level - high).astype(jnp.bfloat16).astype(jnp.float32)
            low = level - high - middle
            three = jnp.where(lane < 32, high, jnp.where(lane < 64, middle, low))
            for half in (0, 1):
                pick = slice(half * HALF, half * HALF + HALF)
                out_ref[chunk + half, :, 0:HEAD_DIM] = summed[pick].astype(jnp.bfloat16)
                out_ref[chunk + half, :, HEAD_DIM:WIDE] = three[pick].astype(jnp.bfloat16)

    each = 2

    def body(i, _):
        for ask in range(asks):
            for sub in range(each):
                step(ask, each * i + sub)
        return 0

    if partner:
        for block in range(4):
            step(0, block)
    else:
        lax.fori_loop(0, 4 // each, body, 0)


def level_of(lanes):
    lanes = lanes.astype(jnp.float32)
    return (lanes[:, 0:1] + lanes[:, 32:33]) + lanes[:, 64:65]


def attend(queries, keys, ids=None, carry=(), final=False, other=None, place=None):
    arrays = [array for array, _, _ in keys]
    operands = [*queries] + ([] if ids is None else [ids]) + arrays + [*carry]
    operands += [] if other is None else [other]
    aliases = {}
    if carry and not final:
        aliases = {len(queries) + len(keys) + i: i for i in range(len(queries))}
    if not final:
        out = jax.ShapeDtypeStruct((1024, WIDE), jnp.float32)
    elif other is None:
        out = shaped(8, HALF, WIDE)
    else:
        out = shaped(8, HALF, HEAD_DIM)
    parts = tuple((start, count) for _, start, count in keys)
    width = sum(count for _, count in parts) * HALF * (1 if ids is None else 2)
    specs = [whole()] * len(operands)
    if other is not None:
        operands, specs = [place] + operands, [scalars()] + specs
    return pl.pallas_call(
        functools.partial(
            attend_kernel, ids is not None, parts, len(queries), len(carry) > 0, final, other is not None
        ),
        out_shape=[out] * len(queries),
        in_specs=specs,
        out_specs=[whole()] * len(queries),
        input_output_aliases=aliases,
        **params(4 * 1024 * len(queries) * width * HEAD_DIM, 4 * MIB, 24),
    )(*operands)


def merge_kernel(part_ref, out_ref):
    levels = [level_of(part_ref[i, :, HEAD_DIM:WIDE]) for i in range(8)]
    top = functools.reduce(jnp.maximum, levels)
    shares = [jnp.exp(level - top) for level in levels]
    summed = sum(
        share * part_ref[i, :, 0:HEAD_DIM].astype(jnp.float32) for i, share in enumerate(shares)
    )
    out_ref[...] = (summed * (1.0 / sum(shares))).astype(jnp.bfloat16)


def merge(part):
    return pl.pallas_call(
        merge_kernel,
        out_shape=shaped(HALF, HEAD_DIM),
        in_specs=[whole()],
        out_specs=whole(),
        **params(0, 2 * MIB),
    )(part)


def per_device(
    enc_query,
    enc_key,
    enc_value,
    input_segments,
    doc_bounds,
    target_query,
    cross_key,
    cross_value,
    target_segments,
):
    del doc_bounds
    ix, iz, ic = lax.axis_index("x"), lax.axis_index("z"), lax.axis_index("core")
    place = jnp.stack([iz, ic, ix]).astype(jnp.int32)
    local = functools.partial(copies, place)
    numbers = input_segments.reshape(2, HALF)
    target_ids = target_segments.reshape(4, 8, TGT).transpose(1, 0, 2).astype(jnp.float32)
    target_ids = jnp.broadcast_to(target_ids.reshape(8, 1, 128), (8, 8, 128))

    spread = jnp.broadcast_to(target_query[None], (8, TGT, 4 * HEAD_DIM))
    spread = lax.all_to_all(spread, "z", 0, 0, tiled=True)
    near, away = load(place, enc_key, enc_value, enc_query)
    swapped = core_swap(away)
    def packed(shifts, after=()):
        plan = functools.partial(plan_pack, shifts)
        return local(plan, [near, swapped, numbers], [(ROWS, HEAD_DIM)] * len(shifts), after)

    sent = packed(ORDER[:5])
    got = [sent[0]] + [z_send(sent[k], ORDER[k]) for k in range(1, 5)]
    heads = load_cross(cross_key, cross_value, numbers, sent[1])
    heads = add_targets(heads, spread, got[3])
    cross = lax.all_to_all(heads, "x", 0, 0, tiled=True)
    group, ask = local(plan_first, got, [(5, KEYS, HEAD_DIM), (5, ASK, HEAD_DIM)], [heads])


    sent = packed(ORDER[5:], [got[3]])
    rest = [z_send(chunk, d) for chunk, d in zip(sent, ORDER[5:], strict=True)]
    left, right = x_send(group, 1), x_send(group, 3)
    to_right, to_left, mine = local(
        plan_second,
        [*rest, left, right, ask],
        [(6, KEYS, HEAD_DIM), (5, KEYS, HEAD_DIM), (8, ASK, HEAD_DIM)],
    )

    from_left, from_right = x_send(to_right, 1), x_send(to_left, 3)
    theirs = core_swap(mine)
    (targets,) = local(plan_targets, [cross], [(8, HALF, HEAD_DIM)], [to_right])
    (part,) = attend([targets], [(cross, 0, 4)], ids=target_ids, final=True)
    part = lax.all_to_all(part, "z", 0, 0, tiled=True)
    queries = (mine, theirs)
    carry = attend(queries, [(group, 0, 5), (to_right, 3, 3), (left, 0, 5), (right, 0, 5)])
    lasts = local(
        plan_third, [from_left, from_right], [(1, KEYS, HEAD_DIM), (2, KEYS, HEAD_DIM)], [carry[0]]
    )

    far = [x_send(lasts[0], 1), x_send(lasts[1], 3)]
    carry = attend(queries, [(from_left, 0, 6), (from_right, 0, 5)], carry=carry)
    far_keys = [(far[0], 0, 1), (far[1], 0, 2)]
    (partial,) = attend([theirs], far_keys, carry=carry[1:], final=True)
    (back,) = attend([mine], far_keys, carry=carry[:1], final=True, other=core_swap(partial), place=place)

    merged = merge(part)
    blocks = local(plan_cross_back, [merged], [(TGT, HEAD_DIM)] * 4, [back])
    blocks = [x_send(b, -d) if d else b for b, d in zip(blocks, X_ORDER, strict=True)]
    back = lax.all_to_all(back, "z", 0, 0, tiled=True)
    (away,) = local(plan_back_swap, [back], [(4, HALF, HEAD_DIM)], blocks)
    (enc_out,) = local(plan_unpack, [back, core_swap(away)], [(2 * HALF, 4 * HEAD_DIM)])
    (cross_out,) = local(plan_cross_unpack, blocks, [(TGT, 4 * HEAD_DIM)])
    return enc_out, cross_out


def solution(mesh):
    shape = mesh.shape
    split = Mesh(
        mesh.devices.reshape(4, shape["ctx"] // 4, shape["head"], shape["dp"]), ("x", "z", "core", "dp")
    )
    tokens = P(("dp", "x", "z"), "core")
    placed = (
        tokens,
        tokens,
        tokens,
        P(("dp", "x", "z")),
        P(("dp", "x", "z"), None),
        tokens,
        tokens,
        tokens,
        P("dp"),
    )
    return jax.shard_map(
        per_device, mesh=split, in_specs=placed, out_specs=(tokens, tokens), check_vma=False
    )
```
